32 devices in a mesh: expert: 2 (over x), dp: 16 (over z, y, core).
Axes of the slice: x: 2, y: 2, z: 4, core: 2. Of those that a mesh axis runs over, the one named last changes fastest.
Arguments:
- x_rows: bfloat16 [2, 16, 2, 2, 3072], P('expert', 'dp'), may hold values from -6 to 6
- cot_rows: bfloat16 [2, 16, 2, 2, 3072], P('expert', 'dp'), may hold values from -3 to 3
- counts: int32 [2, 16, 2], P(None, 'dp'), may hold values from 0 to 2, as said below
- w_gate: bfloat16 [2, 3072, 2048], P('expert', None, 'dp'), may hold values from -0.109375 to 0.109375
- w_up: bfloat16 [2, 3072, 2048], P('expert', None, 'dp'), may hold values from -0.109375 to 0.109375
- w_down: bfloat16 [2, 2048, 3072], P('expert', 'dp'), may hold values from -0.125 to 0.125
- kept_blocks: int32 [2], P('expert'), may hold values from 4 to 16
- block_rank: int32 [2, 16], P('expert', 'dp'), may hold values from 0 to 15, each once within a row
Outputs:
- grad_rows: bfloat16 [2, 16, 2, 2, 3072], P('expert', 'dp')
- grad_gate: bfloat16 [2, 3072, 2048], P('expert', None, 'dp')
- grad_up: bfloat16 [2, 3072, 2048], P('expert', None, 'dp')
- grad_down: bfloat16 [2, 2048, 3072], P('expert', 'dp')
The draws below stay inside these ranges and needn't reach their ends.
Inputs may be any that keep to these rules, and one draw needn't show every extreme that they name: The live slots of a source's buffer for an expert are its first ones. For every expert e and index d the sum over sources s of counts[s, d, e] is at most 4, and it equals 4 for every d of some expert.
All inputs are finite; a program needn't handle non-finite values.
Results may differ from the reference program's by a relative error of at most 0.005.
Values may be sent and summed in bfloat16 or wider, within the bound.
A program may use at most 64 MiB of HBM per device.

```python
import jax
import jax.numpy as jnp

D = 3072
BLOCK = 128
CAP = 2
LIVE = 4
EXPERTS = 2
HIDDEN_SIZE = 2048
N_EXPERT = 2
N_DP = 16


def draw_counts(key, part):
    key = jax.random.fold_in(key, 11)
    key_heavy, key_light, key_order = jax.random.split(key, 3)
    heavy = jax.random.randint(key_heavy, (), 0, EXPERTS)
    light = jax.random.randint(key_light, (EXPERTS, N_DP), 3 * LIVE // 4, LIVE + 1)
    chosen = jnp.arange(EXPERTS)[:, None] == heavy
    load = jnp.where(chosen, LIVE, light)
    scores = jax.random.randint(key_order, (EXPERTS, N_DP, N_EXPERT), 0, 1 << 20) * N_EXPERT + jnp.arange(N_EXPERT)
    order = jnp.argsort(jnp.argsort(scores, axis=-1), axis=-1)
    share = jnp.clip(load[:, :, None] - CAP * order, 0, CAP)
    return jnp.transpose(share, (2, 1, 0)).astype(jnp.int32)


def shard_levels(rng, extent, shards, smallest, top_value):
    factor_of, own = 1.0, jax.random.fold_in(rng, 6)
    for position, parts in shards:
        steps = jnp.exp(jax.random.uniform(jax.random.fold_in(own, position), (parts,), jnp.float32, smallest / len(shards), top_value / len(shards)))
        factor_of = factor_of * jnp.repeat(steps, extent[position] // parts).reshape([-1 if axis == position else 1 for axis in range(len(extent))])
    return factor_of


def centred(key, dims, deviation, limit, pieces=(), held_as=jnp.bfloat16):
    array = jax.random.normal(key, dims, jnp.float32) * deviation
    if len(pieces) > 0:
        array = shard_levels(key, dims, pieces, -0.22, 0.18) * array
    return jnp.clip(array, min=-limit, max=limit).astype(held_as)


def setup_inputs(seed: int = 0) -> dict:
    key_list = jax.random.split(jax.random.key(seed), 9)
    return {
        "x_rows": centred(key_list[0], (N_EXPERT, N_DP, EXPERTS, CAP, D), 1.0, 6.0, ((0, 2), (1, 16))),
        "cot_rows": centred(key_list[1], (N_EXPERT, N_DP, EXPERTS, CAP, D), 0.5, 3.0, ((0, 2), (1, 16))),
        "counts": draw_counts(jax.random.fold_in(key_list[8], 71), 0),
        "w_gate": centred(key_list[3], (EXPERTS, D, HIDDEN_SIZE), D ** -0.5, 0.109375, ((0, 2), (2, 16))),
        "w_up": centred(key_list[4], (EXPERTS, D, HIDDEN_SIZE), D ** -0.5, 0.109375, ((0, 2), (2, 16))),
        "w_down": centred(key_list[5], (EXPERTS, HIDDEN_SIZE, D), HIDDEN_SIZE ** -0.5, 0.125, ((0, 2), (1, 16))),
        "kept_blocks": jax.random.randint(key_list[6], (EXPERTS,), N_DP // 4, N_DP + 1).astype(jnp.int32),
        "block_rank": jax.vmap(lambda own: jax.random.permutation(own, N_DP))(jax.random.split(key_list[7], EXPERTS)).reshape((EXPERTS, N_DP)).astype(jnp.int32),
    }


def compact_matrix(slot_counts, live_rows, capacity):
    sources = slot_counts.shape[0]
    within_slot = jnp.tile(jnp.arange(capacity, dtype=jnp.int32), sources)
    count_slot = jnp.repeat(slot_counts, capacity)
    offsets = jnp.repeat(jnp.cumsum(slot_counts) - slot_counts, capacity)
    target = offsets + within_slot
    alive = within_slot < count_slot
    row_index = jnp.arange(live_rows, dtype=jnp.int32)[:, None]
    return ((row_index == target[None, :]) & alive[None, :]).astype(jnp.bfloat16)


def pack_for(slot_counts):
    return compact_matrix(slot_counts, LIVE, CAP)


def reference(x_rows, cot_rows, counts, w_gate, w_up, w_down, kept_blocks, block_rank):
    row_parts = []
    gate_parts = []
    up_parts = []
    down_parts = []
    for expert_id in range(EXPERTS):
        chooser = jax.vmap(pack_for)(jnp.transpose(counts[:, :, expert_id], (1, 0)))
        chooser_f = chooser.astype(jnp.float32)
        slot_rows = jnp.transpose(x_rows[:, :, expert_id], (1, 0, 2, 3)).reshape(N_DP, N_EXPERT * CAP, D)
        slot_cots = jnp.transpose(cot_rows[:, :, expert_id], (1, 0, 2, 3)).reshape(N_DP, N_EXPERT * CAP, D)
        packed = jnp.einsum("dls,dsc->dlc", chooser_f, slot_rows.astype(jnp.float32)).astype(jnp.bfloat16)
        packed_cots = jnp.einsum("dls,dsc->dlc", chooser_f, slot_cots.astype(jnp.float32)).astype(jnp.bfloat16)
        packed = packed.reshape(N_DP * LIVE, D)
        packed_cots = packed_cots.reshape(N_DP * LIVE, D)
        keep_mask = jnp.repeat((block_rank[expert_id] < kept_blocks[expert_id]).astype(jnp.float32), BLOCK)
        gate_pre = jnp.dot(packed, w_gate[expert_id], preferred_element_type=jnp.float32)
        up_pre = jnp.dot(packed, w_up[expert_id], preferred_element_type=jnp.float32)
        sigmoid_gate = jax.nn.sigmoid(gate_pre)
        activated = gate_pre * sigmoid_gate
        hidden = (activated * up_pre * keep_mask).astype(jnp.bfloat16)
        hidden_grad = jnp.dot(packed_cots, w_down[expert_id].T, preferred_element_type=jnp.float32)
        up_grad = (hidden_grad * activated * keep_mask).astype(jnp.bfloat16)
        gate_grad = (hidden_grad * up_pre * sigmoid_gate * (1.0 + gate_pre * (1.0 - sigmoid_gate)) * keep_mask).astype(jnp.bfloat16)
        down_parts.append(jnp.dot(hidden.T, packed_cots, preferred_element_type=jnp.float32).astype(jnp.bfloat16))
        gate_parts.append(jnp.dot(packed.T, gate_grad, preferred_element_type=jnp.float32).astype(jnp.bfloat16))
        up_parts.append(jnp.dot(packed.T, up_grad, preferred_element_type=jnp.float32).astype(jnp.bfloat16))
        row_grads = jnp.dot(gate_grad, w_gate[expert_id].T, preferred_element_type=jnp.float32)
        row_grads = row_grads + jnp.dot(up_grad, w_up[expert_id].T, preferred_element_type=jnp.float32)
        row_grads = row_grads.astype(jnp.bfloat16).reshape(N_DP, LIVE, D)
        slot_grads = jnp.einsum("dls,dlc->dsc", chooser_f, row_grads.astype(jnp.float32)).astype(jnp.bfloat16)
        row_parts.append(slot_grads.reshape(N_DP, N_EXPERT, CAP, D))
    grad_rows = jnp.transpose(jnp.stack(row_parts), (2, 1, 0, 3, 4))
    return grad_rows, jnp.stack(gate_parts), jnp.stack(up_parts), jnp.stack(down_parts)
```

```python
import jax
import jax.numpy as jnp
from jax import lax
from jax.experimental import pallas as pl
from jax.experimental.pallas import tpu as pltpu
from jax.sharding import PartitionSpec as P

LIVE = 4


def compact_matrix(slot_counts, live_rows, capacity):
    sources = slot_counts.shape[0]
    within_slot = jnp.tile(jnp.arange(capacity, dtype=jnp.int32), sources)
    count_slot = jnp.repeat(slot_counts, capacity)
    offsets = jnp.repeat(jnp.cumsum(slot_counts) - slot_counts, capacity)
    target = offsets + within_slot
    alive = within_slot < count_slot
    row_index = jnp.arange(live_rows, dtype=jnp.int32)[:, None]
    return ((row_index == target[None, :]) & alive[None, :]).astype(jnp.bfloat16)


def contract(left, right, left_dim, right_dim):
    return lax.dot_general(
        left, right, (((left_dim,), (right_dim,)), ((), ())), preferred_element_type=jnp.float32
    )


def body(x_rows, cot_rows, counts, w_gate, w_up, w_down, kept_blocks, block_rank):
    expert_count = x_rows.shape[2]
    capacity = x_rows.shape[3]
    model_width = x_rows.shape[4]
    slot_rows = x_rows.reshape(expert_count, capacity, model_width)
    slot_cots = cot_rows.reshape(expert_count, capacity, model_width)
    my_expert = lax.axis_index("expert")
    picked = jnp.arange(expert_count, dtype=jnp.int32)[None, :] == my_expert
    own_counts = jnp.sum(jnp.where(picked, counts[:, 0, :], 0), axis=1)
    chooser = compact_matrix(own_counts, LIVE, capacity)

    def pack_rows(received):
        flat_rows = received.reshape(-1, model_width)
        return jnp.dot(chooser, flat_rows, preferred_element_type=jnp.float32).astype(jnp.bfloat16)

    got_rows, got_cots = (
        lax.all_to_all(slot_rows, "expert", split_axis=0, concat_axis=0, tiled=True),
        lax.all_to_all(slot_cots, "expert", split_axis=0, concat_axis=0, tiled=True),
    )
    group_rows, group_cots = (
        lax.all_gather(pack_rows(got_rows), "dp", axis=0, tiled=True),
        lax.all_gather(pack_rows(got_cots), "dp", axis=0, tiled=True),
    )
    gate_weight = w_gate[0]
    up_weight = w_up[0]
    down_weight = w_down[0]
    keep_mask = (block_rank.reshape(()) < kept_blocks.reshape(())).astype(jnp.float32)
    gate_pre = jnp.dot(group_rows, gate_weight, preferred_element_type=jnp.float32)
    up_pre = jnp.dot(group_rows, up_weight, preferred_element_type=jnp.float32)
    sigmoid_gate = jax.nn.sigmoid(gate_pre)
    activated = gate_pre * sigmoid_gate
    hidden = (activated * up_pre * keep_mask).astype(jnp.bfloat16)
    hidden_grad = contract(group_cots, down_weight, 1, 1)
    up_grad = (hidden_grad * activated * keep_mask).astype(jnp.bfloat16)
    gate_grad = (
        hidden_grad * up_pre * sigmoid_gate * (1.0 + gate_pre * (1.0 - sigmoid_gate)) * keep_mask
    ).astype(jnp.bfloat16)
    grad_down = contract(hidden, group_cots, 0, 0).astype(jnp.bfloat16)
    grad_gate = contract(group_rows, gate_grad, 0, 0).astype(jnp.bfloat16)
    grad_up = contract(group_rows, up_grad, 0, 0).astype(jnp.bfloat16)
    whole_term = contract(gate_grad, gate_weight, 1, 1) + contract(up_grad, up_weight, 1, 1)
    row_grads = lax.psum_scatter(whole_term, "dp", scatter_dimension=0, tiled=True)
    row_grads = row_grads.astype(jnp.bfloat16)
    slot_grads = contract(chooser, row_grads, 0, 0).astype(jnp.bfloat16)
    slot_grads = slot_grads.reshape(expert_count, capacity, model_width)
    returned = lax.all_to_all(slot_grads, "expert", split_axis=0, concat_axis=0, tiled=True)
    grad_rows = returned.reshape(1, 1, expert_count, capacity, model_width)
    return (grad_rows, grad_gate[None], grad_up[None], grad_down[None])


def exchange_kernel(
    prep_ref, counts_ref, kept_ref, rank_ref, wg_ref, wu_ref, wd_ref,
    rows_out, gate_out, up_out, down_out,
    stage, landed, rows, w_in, w_down, acc_gu, acc_dh, sib_out, sib_in, part, unit, unit_in,
    final_out, final_in, grad_in, grad_down,
    s1_send, s1_recv, z_send, z_recv, y_send, y_recv, sb_send, sb_recv,
    r1_send, r1_recv, r2_send, r2_recv, f_send, f_recv, load_sem, store_sem,
):
    s = lax.axis_index("expert")
    d = lax.axis_index("dp")
    z, y, c = d // 4, (d // 2) % 2, d % 2
    width = rows.shape[1]
    half = width // 2
    quarter = half // 4
    pair = half // 2

    def device(e, zz, yy, cc):
        return (e, zz * 4 + yy * 2 + cc)

    def remote(src, dst, send, recv, where):
        return pltpu.make_async_remote_copy(
            src_ref=src, dst_ref=dst, send_sem=send, recv_sem=recv, device_id=where,
            device_id_type=pl.DeviceIdType.MESH,
        )

    near = [(0, 1), (1, 0), (1, 1)]
    chips = [(dz, dy) for dz in range(4) for dy in range(2) if (dz, dy) != (0, 0)]

    def near_device(de, dc):
        return device((s + de) % 2, z, y, (c + dc) % 2)

    def chip_device(dz, dy):
        return device(s, (z + dz) % 4, (y + dy) % 2, c)

    loads = [
        pltpu.make_async_copy(wg_ref.at[0], w_in.at[:, pl.ds(0, 128)], load_sem.at[0]),
        pltpu.make_async_copy(wu_ref.at[0], w_in.at[:, pl.ds(128, 128)], load_sem.at[1]),
        pltpu.make_async_copy(wd_ref.at[0], w_down, load_sem.at[2]),
    ]
    barrier = pltpu.get_barrier_semaphore()
    for de, dc in near:
        pl.semaphore_signal(barrier, inc=1, device_id=near_device(de, dc), device_id_type=pl.DeviceIdType.MESH)
    for dz, dy in chips:
        pl.semaphore_signal(barrier, inc=1, device_id=chip_device(dz, dy), device_id_type=pl.DeviceIdType.MESH)
    for load in loads:
        load.start()

    row16 = lax.broadcasted_iota(jnp.int32, (16, quarter), 0)
    slot = (row16 >> 2) & 1
    for e in range(2):
        live = jnp.where(s == 0, counts_ref[0, 0, e], counts_ref[1, 0, e])
        for h in range(2):
            value = prep_ref[e, h].astype(jnp.float32)
            stage[e, h] = jnp.where(slot < live, value, 0.0).astype(jnp.bfloat16)

    i = lax.broadcasted_iota(jnp.int32, (64, 64), 0)
    j = lax.broadcasted_iota(jnp.int32, (64, 64), 1)
    order = (
        ((i >> 4) == (j & 3))
        & (((i >> 3) & 1) == ((j >> 3) & 1))
        & (((i >> 2) & 1) == ((j >> 5) & 1))
        & (((i >> 1) & 1) == ((j >> 4) & 1))
        & ((i & 1) == ((j >> 2) & 1))
    ).astype(jnp.float32).astype(jnp.bfloat16)
    oi = lax.broadcasted_iota(jnp.int32, (16, 64), 0)
    oj = lax.broadcasted_iota(jnp.int32, (16, 64), 1)
    chosen = (
        ((oi >> 3) == (oj >> 5))
        & (((oi >> 2) & 1) == (oj & 1))
        & (((oi >> 1) & 1) == ((oj >> 4) & 1))
        & ((oi & 1) == ((oj >> 3) & 1))
        & (((oj >> 2) & 1) == c)
        & (((oj >> 1) & 1) == s)
    ).astype(jnp.float32).astype(jnp.bfloat16)

    pl.semaphore_wait(barrier, len(near) + len(chips))

    mine = pl.ds(pl.multiple_of((c * 2 + s) * 16, 16), 16)
    sends = []
    first = []
    for de, dc in near:
        index = de * 2 + dc
        copy = remote(
            stage.at[(s + de) % 2, (c + dc) % 2], landed.at[mine, :], s1_send.at[index], s1_recv.at[index],
            near_device(de, dc),
        )
        copy.start()
        first.append(copy)
    landed[mine, :] = stage[s, c]
    for copy in first:
        copy.wait_recv()
    sends += first

    def block(zz, yy, hh):
        return rows.at[
            pl.ds(pl.multiple_of((yy * 4 + zz) * 16, 16), 16), pl.ds(pl.multiple_of(hh * half, 128), half)
        ]

    ordered = jnp.dot(order, landed[...], preferred_element_type=jnp.float32).astype(jnp.bfloat16)
    my_rows = pl.ds(pl.multiple_of((y * 4 + z) * 16, 16), 16)
    for g in range(4):
        rows[my_rows, pl.ds(pl.multiple_of(c * half + g * quarter, 128), quarter)] = ordered[g * 16:(g + 1) * 16, :]

    def forward(ref, send, recv, where):
        copy = remote(ref, ref, send, recv, where)
        copy.start()
        sends.append(copy)
        return copy

    sibling = device(s, z, y, 1 - c)
    opposite = device(s, z, 1 - y, c)
    own = block(z, y, c)
    z_copies = {}
    for dz in (2, 1, 3):
        z_copies[dz] = forward(own, z_send.at[dz - 1], z_recv.at[dz - 1], device(s, (z + dz) % 4, y, c))
    y_copies = [forward(own, y_send.at[0], y_recv.at[0], opposite)]
    s_copies = [forward(own, sb_send.at[0], sb_recv.at[0], sibling)]
    for dz in (1, 3, 2):
        z_copies[dz].wait_recv()
        got = block((z + 4 - dz) % 4, y, c)
        y_copies.append(forward(got, y_send.at[dz], y_recv.at[dz], opposite))
        s_copies.append(forward(got, sb_send.at[dz], sb_recv.at[dz], sibling))

    for load in loads:
        load.wait()

    def inward(yy):
        block_rows = rows[pl.ds(pl.multiple_of(yy * 64, 64), 64), :]
        both = jnp.dot(block_rows, w_in[...], preferred_element_type=jnp.float32)
        acc_gu[pl.ds(pl.multiple_of(yy * 32, 32), 32), :] = both.reshape(4, 16, 256)[:, 0:8].reshape(32, 256)

    def back(yy):
        block_rows = rows[pl.ds(pl.multiple_of(yy * 64, 64), 64), :]
        out = lax.dot_general(block_rows, w_down[...], (((1,), (1,)), ((), ())), preferred_element_type=jnp.float32)
        acc_dh[pl.ds(pl.multiple_of(yy * 32, 32), 32), :] = out.reshape(4, 16, 128)[:, 8:16].reshape(32, 128)

    for copy in s_copies:
        copy.wait_recv()
    inward(y)
    last = []
    for n, dz in enumerate((0, 1, 3, 2)):
        y_copies[n].wait_recv()
        got = block((z + 4 - dz) % 4, 1 - y, c)
        last.append(forward(got, sb_send.at[4 + dz], sb_recv.at[4 + dz], sibling))
    back(y)
    for copy in last:
        copy.wait_recv()
    inward(1 - y)
    back(1 - y)

    keep = jnp.where(rank_ref[0, 0] < kept_ref[0], 1.0, 0.0).astype(jnp.float32)
    gate_pre = acc_gu[:, 0:128]
    up_pre = acc_gu[:, 128:256]
    hidden_grad = acc_dh[...]
    sigmoid_gate = jax.nn.sigmoid(gate_pre)
    activated = gate_pre * sigmoid_gate
    hidden = activated * up_pre * keep
    up_grad = hidden_grad * activated * keep
    gate_grad = hidden_grad * up_pre * sigmoid_gate * (1.0 + gate_pre * (1.0 - sigmoid_gate)) * keep
    both_grad = jnp.concatenate([gate_grad, up_grad], axis=1)
    both_bf16 = both_grad.astype(jnp.bfloat16)

    def partial(hh):
        w_half = w_in[pl.ds(pl.multiple_of(hh * half, 256), half), :]
        term = lax.dot_general(both_bf16, w_half, (((1,), (1,)), ((), ())), preferred_element_type=jnp.float32)
        low = term[:, :pair].reshape(8, 8, pair)
        high = term[:, pair:].reshape(8, 8, pair)
        return jnp.concatenate([low, high], axis=1).reshape(128, pair)

    sib_out[...] = partial(1 - c).astype(jnp.bfloat16)
    sib_copy = remote(sib_out, sib_in, r1_send, r1_recv, sibling)
    sib_copy.start()
    sends.append(sib_copy)
    part[...] = partial(c)

    zeros = jnp.zeros((8, 8, 128), jnp.float32)
    hidden_pad = jnp.concatenate([zeros, hidden.reshape(8, 8, 128)], axis=1).reshape(128, 128).astype(jnp.bfloat16)
    zeros2 = jnp.zeros((8, 8, 256), jnp.float32)
    both_pad = jnp.concatenate([both_grad.reshape(8, 8, 256), zeros2], axis=1).reshape(128, 256).astype(jnp.bfloat16)

    sib_copy.wait_recv()
    total = part[...] + sib_in[...].astype(jnp.float32)
    part[...] = total
    unit[...] = total.astype(jnp.bfloat16)
    unit_copies = []
    for dz, dy in sorted(chips, key=lambda p: p[0] != 2):
        index = dz * 2 + dy
        target = ((y + dy) % 2) * 4 + (z + dz) % 4
        copy = remote(
            unit.at[pl.ds(pl.multiple_of(target * 16, 16), 16), :], unit_in.at[index],
            r2_send.at[index], r2_recv.at[index], chip_device(dz, dy),
        )
        copy.start()
        sends.append(copy)
        unit_copies.append(copy)

    for n in range(4):
        columns = pl.ds(n * pair, pair)
        some = rows[:, columns]
        grad_down[:, columns] = lax.dot_general(
            hidden_pad, some, (((0,), (0,)), ((), ())), preferred_element_type=jnp.float32
        ).astype(jnp.bfloat16)
        grad_in[columns, :] = lax.dot_general(
            some, both_pad, (((0,), (0,)), ((), ())), preferred_element_type=jnp.float32
        ).astype(jnp.bfloat16)
    stores = [
        pltpu.make_async_copy(grad_down, down_out.at[0], store_sem.at[0]),
        pltpu.make_async_copy(grad_in.at[:, pl.ds(0, 128)], gate_out.at[0], store_sem.at[1]),
        pltpu.make_async_copy(grad_in.at[:, pl.ds(128, 128)], up_out.at[0], store_sem.at[2]),
    ]
    for store in stores:
        store.start()

    for copy in unit_copies:
        copy.wait_recv()
    result = part[my_rows, :]
    for dz, dy in chips:
        result = result + unit_in[dz * 2 + dy].astype(jnp.float32)
    final_out[...] = result.astype(jnp.bfloat16)
    place = pl.ds(pl.multiple_of((s * 2 + c) * 16, 16), 16)
    finals = []
    for de, dc in near:
        index = de * 2 + dc
        copy = remote(final_out, final_in.at[place, :], f_send.at[index], f_recv.at[index], near_device(de, dc))
        copy.start()
        finals.append(copy)
    final_in[place, :] = final_out[...]
    for copy in finals:
        copy.wait_recv()
    sends += finals
    rows_out[...] = jnp.dot(chosen, final_in[...], preferred_element_type=jnp.float32).astype(jnp.bfloat16)
    for copy in sends:
        copy.wait_send()
    for store in stores:
        store.wait()


def kernel_body(x_rows, cot_rows, counts, w_gate, w_up, w_down, kept_blocks, block_rank):
    width = x_rows.shape[4]
    quarter = width // 8
    pair = width // 4

    def cut(slots):
        return jnp.transpose(slots.reshape(2, 2, 2, 4, quarter), (0, 2, 1, 3, 4))

    prep = jnp.stack([cut(x_rows), cut(cot_rows)], axis=2).reshape(2, 2, 16, quarter)
    vmem = pl.BlockSpec(memory_space=pltpu.VMEM)
    smem = pl.BlockSpec(memory_space=pltpu.SMEM)
    hbm = pl.BlockSpec(memory_space=pl.ANY)
    bf16, f32 = jnp.bfloat16, jnp.float32
    dma = pltpu.SemaphoreType.DMA
    out_rows, grad_gate, grad_up, grad_down = pl.pallas_call(
        exchange_kernel,
        out_shape=(
            jax.ShapeDtypeStruct((16, pair), bf16),
            jax.ShapeDtypeStruct(w_gate.shape, bf16),
            jax.ShapeDtypeStruct(w_up.shape, bf16),
            jax.ShapeDtypeStruct(w_down.shape, bf16),
        ),
        in_specs=[vmem, smem, smem, smem, hbm, hbm, hbm],
        out_specs=(vmem, hbm, hbm, hbm),
        scratch_shapes=[
            pltpu.VMEM((2, 2, 16, quarter), bf16),
            pltpu.VMEM((64, quarter), bf16),
            pltpu.VMEM((128, width), bf16),
            pltpu.VMEM((width, 256), bf16),
            pltpu.VMEM((128, width), bf16),
            pltpu.VMEM((64, 256), f32),
            pltpu.VMEM((64, 128), f32),
            pltpu.VMEM((128, pair), bf16),
            pltpu.VMEM((128, pair), bf16),
            pltpu.VMEM((128, pair), f32),
            pltpu.VMEM((128, pair), bf16),
            pltpu.VMEM((8, 16, pair), bf16),
            pltpu.VMEM((16, pair), bf16),
            pltpu.VMEM((64, pair), bf16),
            pltpu.VMEM((width, 256), bf16),
            pltpu.VMEM((128, width), bf16),
            dma((4,)), dma((4,)), dma((3,)), dma((3,)), dma((4,)), dma((4,)), dma((8,)), dma((8,)),
            dma(()), dma(()), dma((8,)), dma((8,)), dma((4,)), dma((4,)), dma((3,)), dma((3,)),
        ],
        compiler_params=pltpu.CompilerParams(
            collective_id=0, has_side_effects=True, vmem_limit_bytes=32 * 1024 * 1024
        ),
        name="expert_backward",
    )(prep, counts, kept_blocks, block_rank, w_gate, w_up, w_down)
    return (out_rows.reshape(x_rows.shape), grad_gate, grad_up, grad_down)


def solution(mesh):
    in_specs = (
        P("expert", "dp", None, None, None),
        P("expert", "dp", None, None, None),
        P(None, "dp", None),
        P("expert", None, "dp"),
        P("expert", None, "dp"),
        P("expert", "dp", None),
        P("expert"),
        P("expert", "dp"),
    )
    out_specs = (
        P("expert", "dp", None, None, None),
        P("expert", None, "dp"),
        P("expert", None, "dp"),
        P("expert", "dp", None),
    )
    small = mesh.shape["expert"] == 2 and mesh.shape["dp"] == 16
    return jax.shard_map(kernel_body if small else body, mesh=mesh, in_specs=in_specs, out_specs=out_specs, check_vma=False)
```

```python
import jax
import jax.numpy as jnp
from jax import lax
from jax.experimental import pallas as pl
from jax.experimental.pallas import tpu as pltpu
from jax.sharding import PartitionSpec as P

LIVE = 4


def compact_matrix(slot_counts, live_rows, capacity):
    sources = slot_counts.shape[0]
    within_slot = jnp.tile(jnp.arange(capacity, dtype=jnp.int32), sources)
    count_slot = jnp.repeat(slot_counts, capacity)
    offsets = jnp.repeat(jnp.cumsum(slot_counts) - slot_counts, capacity)
    target = offsets + within_slot
    alive = within_slot < count_slot
    row_index = jnp.arange(live_rows, dtype=jnp.int32)[:, None]
    return ((row_index == target[None, :]) & alive[None, :]).astype(jnp.bfloat16)


def contract(left, right, left_dim, right_dim):
    return lax.dot_general(
        left, right, (((left_dim,), (right_dim,)), ((), ())), preferred_element_type=jnp.float32
    )


def body(x_rows, cot_rows, counts, w_gate, w_up, w_down, kept_blocks, block_rank):
    expert_count = x_rows.shape[2]
    capacity = x_rows.shape[3]
    model_width = x_rows.shape[4]
    slot_rows = x_rows.reshape(expert_count, capacity, model_width)
    slot_cots = cot_rows.reshape(expert_count, capacity, model_width)
    my_expert = lax.axis_index("expert")
    picked = jnp.arange(expert_count, dtype=jnp.int32)[None, :] == my_expert
    own_counts = jnp.sum(jnp.where(picked, counts[:, 0, :], 0), axis=1)
    chooser = compact_matrix(own_counts, LIVE, capacity)

    def pack_rows(received):
        flat_rows = received.reshape(-1, model_width)
        return jnp.dot(chooser, flat_rows, preferred_element_type=jnp.float32).astype(jnp.bfloat16)

    got_rows, got_cots = (
        lax.all_to_all(slot_rows, "expert", split_axis=0, concat_axis=0, tiled=True),
        lax.all_to_all(slot_cots, "expert", split_axis=0, concat_axis=0, tiled=True),
    )
    group_rows, group_cots = (
        lax.all_gather(pack_rows(got_rows), "dp", axis=0, tiled=True),
        lax.all_gather(pack_rows(got_cots), "dp", axis=0, tiled=True),
    )
    gate_weight = w_gate[0]
    up_weight = w_up[0]
    down_weight = w_down[0]
    keep_mask = (block_rank.reshape(()) < kept_blocks.reshape(())).astype(jnp.float32)
    gate_pre = jnp.dot(group_rows, gate_weight, preferred_element_type=jnp.float32)
    up_pre = jnp.dot(group_rows, up_weight, preferred_element_type=jnp.float32)
    sigmoid_gate = jax.nn.sigmoid(gate_pre)
    activated = gate_pre * sigmoid_gate
    hidden = (activated * up_pre * keep_mask).astype(jnp.bfloat16)
    hidden_grad = contract(group_cots, down_weight, 1, 1)
    up_grad = (hidden_grad * activated * keep_mask).astype(jnp.bfloat16)
    gate_grad = (
        hidden_grad * up_pre * sigmoid_gate * (1.0 + gate_pre * (1.0 - sigmoid_gate)) * keep_mask
    ).astype(jnp.bfloat16)
    grad_down = contract(hidden, group_cots, 0, 0).astype(jnp.bfloat16)
    grad_gate = contract(group_rows, gate_grad, 0, 0).astype(jnp.bfloat16)
    grad_up = contract(group_rows, up_grad, 0, 0).astype(jnp.bfloat16)
    whole_term = contract(gate_grad, gate_weight, 1, 1) + contract(up_grad, up_weight, 1, 1)
    row_grads = lax.psum_scatter(whole_term, "dp", scatter_dimension=0, tiled=True)
    row_grads = row_grads.astype(jnp.bfloat16)
    slot_grads = contract(chooser, row_grads, 0, 0).astype(jnp.bfloat16)
    slot_grads = slot_grads.reshape(expert_count, capacity, model_width)
    returned = lax.all_to_all(slot_grads, "expert", split_axis=0, concat_axis=0, tiled=True)
    grad_rows = returned.reshape(1, 1, expert_count, capacity, model_width)
    return (grad_rows, grad_gate[None], grad_up[None], grad_down[None])


def exchange_kernel(
    x_ref, cot_ref, counts_hbm, kept_ref, rank_ref, wg_ref, wu_ref, wd_ref,
    final_in, gate_out, up_out, down_out,
    slots, counts_ref,
    stage, landed, rows, w_in, w_down, acc_gu, acc_dh, sib_out, sib_in, part, unit, unit_in, final_out,
    s1_send, s1_recv, z_send, z_recv, y_send, y_recv, sb_send, sb_recv,
    r1_send, r1_recv, r2_send, r2_recv, f_send, f_recv, load_sem, slot_sem,
):
    s = lax.axis_index("expert")
    d = lax.axis_index("dp")
    z, y, c = d // 4, (d // 2) % 2, d % 2
    width = rows.shape[1]
    half = width // 2
    quarter = half // 4
    pair = half // 2

    def device(e, zz, yy, cc):
        return (e, zz * 4 + yy * 2 + cc)

    def remote(src, dst, send, recv, where):
        return pltpu.make_async_remote_copy(
            src_ref=src, dst_ref=dst, send_sem=send, recv_sem=recv, device_id=where,
            device_id_type=pl.DeviceIdType.MESH,
        )

    near = [(0, 1), (1, 0), (1, 1)]
    chips = [(dz, dy) for dz in range(4) for dy in range(2) if (dz, dy) != (0, 0)]

    def near_device(de, dc):
        return device((s + de) % 2, z, y, (c + dc) % 2)

    def chip_device(dz, dy):
        return device(s, (z + dz) % 4, (y + dy) % 2, c)

    slot_loads = [
        pltpu.make_async_copy(x_ref.at[0, 0], slots.at[0], slot_sem.at[0]),
        pltpu.make_async_copy(cot_ref.at[0, 0], slots.at[1], slot_sem.at[1]),
        pltpu.make_async_copy(counts_hbm, counts_ref, slot_sem.at[2]),
    ]
    loads = [
        pltpu.make_async_copy(wg_ref.at[0], w_in.at[:, pl.ds(0, 128)], load_sem.at[0]),
        pltpu.make_async_copy(wu_ref.at[0], w_in.at[:, pl.ds(128, 128)], load_sem.at[1]),
        pltpu.make_async_copy(wd_ref.at[0], w_down, load_sem.at[2]),
    ]
    barrier = pltpu.get_barrier_semaphore()
    for de, dc in near:
        pl.semaphore_signal(barrier, inc=1, device_id=near_device(de, dc), device_id_type=pl.DeviceIdType.MESH)
    for dz, dy in chips:
        pl.semaphore_signal(barrier, inc=1, device_id=chip_device(dz, dy), device_id_type=pl.DeviceIdType.MESH)
    for load in slot_loads + loads:
        load.start()
    for load in slot_loads:
        load.wait()

    row16 = lax.broadcasted_iota(jnp.int32, (16, quarter), 0)
    slot = (row16 >> 2) & 1
    for e in range(2):
        live = jnp.where(s == 0, counts_ref[0, 0, e], counts_ref[1, 0, e])
        sources = [slots[0, e].astype(jnp.float32), slots[1, e].astype(jnp.float32)]
        for h in range(2):
            value = jnp.zeros((16, quarter), jnp.float32)
            for r in range(16):
                t, k, g = r // 8, (r // 4) % 2, r % 4
                start = h * half + g * quarter
                line = sources[t][k:k + 1, start:start + quarter]
                value = jnp.where(row16 == r, jnp.broadcast_to(line, value.shape), value)
            stage[e, h] = jnp.where(slot < live, value, 0.0).astype(jnp.bfloat16)

    i = lax.broadcasted_iota(jnp.int32, (64, 64), 0)
    j = lax.broadcasted_iota(jnp.int32, (64, 64), 1)
    order = (
        ((i >> 4) == (j & 3))
        & (((i >> 3) & 1) == ((j >> 3) & 1))
        & (((i >> 2) & 1) == ((j >> 5) & 1))
        & (((i >> 1) & 1) == ((j >> 4) & 1))
        & ((i & 1) == ((j >> 2) & 1))
    ).astype(jnp.float32).astype(jnp.bfloat16)

    pl.semaphore_wait(barrier, len(near) + len(chips))

    mine = pl.ds(pl.multiple_of((c * 2 + s) * 16, 16), 16)
    sends = []
    first = []
    for de, dc in near:
        index = de * 2 + dc
        copy = remote(
            stage.at[(s + de) % 2, (c + dc) % 2], landed.at[mine, :], s1_send.at[index], s1_recv.at[index],
            near_device(de, dc),
        )
        copy.start()
        first.append(copy)
    landed[mine, :] = stage[s, c]
    for copy in first:
        copy.wait_recv()
    sends += first

    def block(zz, yy, hh):
        return rows.at[
            pl.ds(pl.multiple_of((yy * 4 + zz) * 16, 16), 16), pl.ds(pl.multiple_of(hh * half, 128), half)
        ]

    ordered = jnp.dot(order, landed[...], preferred_element_type=jnp.float32).astype(jnp.bfloat16)
    my_rows = pl.ds(pl.multiple_of((y * 4 + z) * 16, 16), 16)
    for g in range(4):
        rows[my_rows, pl.ds(pl.multiple_of(c * half + g * quarter, 128), quarter)] = ordered[g * 16:(g + 1) * 16, :]

    def forward(ref, send, recv, where):
        copy = remote(ref, ref, send, recv, where)
        copy.start()
        sends.append(copy)
        return copy

    sibling = device(s, z, y, 1 - c)
    opposite = device(s, z, 1 - y, c)
    own = block(z, y, c)
    z_copies = {}
    for dz in (2, 1, 3):
        z_copies[dz] = forward(own, z_send.at[dz - 1], z_recv.at[dz - 1], device(s, (z + dz) % 4, y, c))
    y_copies = [forward(own, y_send.at[0], y_recv.at[0], opposite)]
    s_copies = [forward(own, sb_send.at[0], sb_recv.at[0], sibling)]
    for dz in (1, 3, 2):
        z_copies[dz].wait_recv()
        got = block((z + 4 - dz) % 4, y, c)
        y_copies.append(forward(got, y_send.at[dz], y_recv.at[dz], opposite))
        s_copies.append(forward(got, sb_send.at[dz], sb_recv.at[dz], sibling))

    for load in loads:
        load.wait()

    def forward_part(yy, hh, start):
        columns = pl.ds(pl.multiple_of(hh * half, 256), half)
        some = rows[pl.ds(pl.multiple_of(yy * 64, 64), 64), columns]
        both = jnp.dot(some, w_in[columns, :], preferred_element_type=jnp.float32)
        back = lax.dot_general(
            some, w_down[:, columns], (((1,), (1,)), ((), ())), preferred_element_type=jnp.float32
        )
        both = both.reshape(4, 16, 256)[:, 0:8].reshape(32, 256)
        back = back.reshape(4, 16, 128)[:, 8:16].reshape(32, 128)
        place = pl.ds(pl.multiple_of(yy * 32, 32), 32)
        if not start:
            both = both + acc_gu[place, :]
            back = back + acc_dh[place, :]
        acc_gu[place, :] = both
        acc_dh[place, :] = back

    last = []

    def pass_on(n, dz):
        y_copies[n].wait_recv()
        got = block((z + 4 - dz) % 4, 1 - y, c)
        last.append(forward(got, sb_send.at[4 + dz], sb_recv.at[4 + dz], sibling))

    forward_part(y, c, True)
    pass_on(0, 0)
    for copy in s_copies:
        copy.wait_recv()
    forward_part(y, 1 - c, False)
    for n, dz in ((1, 1), (2, 3), (3, 2)):
        pass_on(n, dz)
    forward_part(1 - y, c, True)
    for copy in last:
        copy.wait_recv()
    forward_part(1 - y, 1 - c, False)

    keep = jnp.where(rank_ref[0, 0] < kept_ref[0], 1.0, 0.0).astype(jnp.float32)
    gate_pre = acc_gu[:, 0:128]
    up_pre = acc_gu[:, 128:256]
    hidden_grad = acc_dh[...]
    sigmoid_gate = jax.nn.sigmoid(gate_pre)
    activated = gate_pre * sigmoid_gate
    hidden = activated * up_pre * keep
    up_grad = hidden_grad * activated * keep
    gate_grad = hidden_grad * up_pre * sigmoid_gate * (1.0 + gate_pre * (1.0 - sigmoid_gate)) * keep
    both_grad = jnp.concatenate([gate_grad, up_grad], axis=1)
    both_bf16 = both_grad.astype(jnp.bfloat16)

    def partial(hh):
        w_half = w_in[pl.ds(pl.multiple_of(hh * half, 256), half), :]
        term = lax.dot_general(both_bf16, w_half, (((1,), (1,)), ((), ())), preferred_element_type=jnp.float32)
        low = term[:, :pair].reshape(8, 8, pair)
        high = term[:, pair:].reshape(8, 8, pair)
        return jnp.concatenate([low, high], axis=1).reshape(128, pair)

    sib_out[...] = partial(1 - c).astype(jnp.bfloat16)
    sib_copy = remote(sib_out, sib_in, r1_send, r1_recv, sibling)
    sib_copy.start()
    sends.append(sib_copy)
    part[...] = partial(c)

    zeros = jnp.zeros((8, 8, 128), jnp.float32)
    hidden_pad = jnp.concatenate([zeros, hidden.reshape(8, 8, 128)], axis=1).reshape(128, 128).astype(jnp.bfloat16)
    zeros2 = jnp.zeros((8, 8, 256), jnp.float32)
    both_pad = jnp.concatenate([both_grad.reshape(8, 8, 256), zeros2], axis=1).reshape(128, 256).astype(jnp.bfloat16)

    sib_copy.wait_recv()
    total = part[...] + sib_in[...].astype(jnp.float32)
    part[...] = total
    unit[...] = total.astype(jnp.bfloat16)
    unit_copies = []
    for dz, dy in sorted(chips, key=lambda p: p[0] != 2):
        index = dz * 2 + dy
        target = ((y + dy) % 2) * 4 + (z + dz) % 4
        copy = remote(
            unit.at[pl.ds(pl.multiple_of(target * 16, 16), 16), :], unit_in.at[index],
            r2_send.at[index], r2_recv.at[index], chip_device(dz, dy),
        )
        copy.start()
        sends.append(copy)
        unit_copies.append(copy)

    for n in range(4):
        columns = pl.ds(n * pair, pair)
        some = rows[:, columns]
        down_out[0, :, columns] = lax.dot_general(
            hidden_pad, some, (((0,), (0,)), ((), ())), preferred_element_type=jnp.float32
        ).astype(jnp.bfloat16)
        inner = lax.dot_general(
            some, both_pad, (((0,), (0,)), ((), ())), preferred_element_type=jnp.float32
        ).astype(jnp.bfloat16)
        gate_out[0, columns, :] = inner[:, 0:128]
        up_out[0, columns, :] = inner[:, 128:256]

    for copy in unit_copies:
        copy.wait_recv()
    result = part[my_rows, :]
    for dz, dy in chips:
        result = result + unit_in[dz * 2 + dy].astype(jnp.float32)
    final_out[...] = result.astype(jnp.bfloat16)
    place = pl.ds(pl.multiple_of((s * 2 + c) * 16, 16), 16)
    finals = []
    for de, dc in near:
        index = de * 2 + dc
        copy = remote(final_out, final_in.at[place, :], f_send.at[index], f_recv.at[index], near_device(de, dc))
        copy.start()
        finals.append(copy)
    final_in[place, :] = final_out[...]
    for copy in finals:
        copy.wait_recv()
    sends += finals
    for copy in sends:
        copy.wait_send()


def finish_kernel(final_ref, gate_ref, up_ref, down_ref, rows_out, gate_out, up_out, down_out, sem):
    copies = [
        pltpu.make_async_copy(gate_ref, gate_out, sem.at[0]),
        pltpu.make_async_copy(up_ref, up_out, sem.at[1]),
        pltpu.make_async_copy(down_ref, down_out, sem.at[2]),
    ]
    for copy in copies:
        copy.start()
    s = lax.axis_index("expert")
    c = lax.axis_index("dp") % 2
    pair = final_ref.shape[1]
    i = lax.broadcasted_iota(jnp.int32, (16, 64), 0)
    j = lax.broadcasted_iota(jnp.int32, (16, 64), 1)
    chosen = (
        ((i >> 3) == (j >> 5))
        & (((i >> 2) & 1) == ((j >> 4) & 1))
        & (((i >> 1) & 1) == ((j >> 3) & 1))
        & ((i & 1) == (j & 1))
        & (((j >> 2) & 1) == c)
        & (((j >> 1) & 1) == s)
    ).astype(jnp.float32).astype(jnp.bfloat16)
    picked = jnp.dot(chosen, final_ref[...], preferred_element_type=jnp.float32)
    for e in range(2):
        for g in range(4):
            start = e * 8 + g * 2
            rows_out[0, 0, e, :, g * pair:(g + 1) * pair] = picked[start:start + 2, :].astype(jnp.bfloat16)
    for copy in copies:
        copy.wait()


def kernel_body(x_rows, cot_rows, counts, w_gate, w_up, w_down, kept_blocks, block_rank):
    width = x_rows.shape[4]
    quarter = width // 8
    pair = width // 4

    vmem = pl.BlockSpec(memory_space=pltpu.VMEM)
    hbm = pl.BlockSpec(memory_space=pltpu.HBM)
    anywhere = pl.BlockSpec(memory_space=pl.ANY)
    smem = pl.BlockSpec(memory_space=pltpu.SMEM)
    held = [
        pltpu.with_memory_space_constraint(a, pltpu.HBM) for a in (x_rows, cot_rows, counts, w_gate, w_up, w_down)
    ]
    bf16, f32 = jnp.bfloat16, jnp.float32
    dma = pltpu.SemaphoreType.DMA
    final_rows, grad_gate, grad_up, grad_down = pl.pallas_call(
        exchange_kernel,
        out_shape=(
            jax.ShapeDtypeStruct((64, pair), bf16),
            jax.ShapeDtypeStruct(w_gate.shape, bf16),
            jax.ShapeDtypeStruct(w_up.shape, bf16),
            jax.ShapeDtypeStruct(w_down.shape, bf16),
        ),
        in_specs=[hbm, hbm, hbm, smem, smem, hbm, hbm, hbm],
        out_specs=(vmem, vmem, vmem, vmem),
        scratch_shapes=[
            pltpu.VMEM((2,) + x_rows.shape[2:], bf16),
            pltpu.SMEM(counts.shape, jnp.int32),
            pltpu.VMEM((2, 2, 16, quarter), bf16),
            pltpu.VMEM((64, quarter), bf16),
            pltpu.VMEM((128, width), bf16),
            pltpu.VMEM((width, 256), bf16),
            pltpu.VMEM((128, width), bf16),
            pltpu.VMEM((64, 256), f32),
            pltpu.VMEM((64, 128), f32),
            pltpu.VMEM((128, pair), bf16),
            pltpu.VMEM((128, pair), bf16),
            pltpu.VMEM((128, pair), f32),
            pltpu.VMEM((128, pair), bf16),
            pltpu.VMEM((8, 16, pair), bf16),
            pltpu.VMEM((16, pair), bf16),
            dma((4,)), dma((4,)), dma((3,)), dma((3,)), dma((4,)), dma((4,)), dma((8,)), dma((8,)),
            dma(()), dma(()), dma((8,)), dma((8,)), dma((4,)), dma((4,)), dma((3,)), dma((3,)),
        ],
        compiler_params=pltpu.CompilerParams(
            collective_id=0, has_side_effects=True, vmem_limit_bytes=32 * 1024 * 1024
        ),
        name="expert_backward",
    )(*held[:3], kept_blocks, block_rank, *held[3:])
    return pl.pallas_call(
        finish_kernel,
        out_shape=tuple(jax.ShapeDtypeStruct(a.shape, bf16) for a in (x_rows, w_gate, w_up, w_down)),
        in_specs=[vmem, anywhere, anywhere, anywhere],
        out_specs=(vmem, anywhere, anywhere, anywhere),
        scratch_shapes=[dma((3,))],
        compiler_params=pltpu.CompilerParams(vmem_limit_bytes=16 * 1024 * 1024),
        name="write_outputs",
    )(final_rows, grad_gate, grad_up, grad_down)


def solution(mesh):
    in_specs = (
        P("expert", "dp", None, None, None),
        P("expert", "dp", None, None, None),
        P(None, "dp", None),
        P("expert", None, "dp"),
        P("expert", None, "dp"),
        P("expert", "dp", None),
        P("expert"),
        P("expert", "dp"),
    )
    out_specs = (
        P("expert", "dp", None, None, None),
        P("expert", None, "dp"),
        P("expert", None, "dp"),
        P("expert", "dp", None),
    )
    small = mesh.shape["expert"] == 2 and mesh.shape["dp"] == 16
    return jax.shard_map(kernel_body if small else body, mesh=mesh, in_specs=in_specs, out_specs=out_specs, check_vma=False)
```

```python
import jax
import jax.numpy as jnp
from jax import lax
from jax.experimental import pallas as pl
from jax.experimental.pallas import tpu as pltpu
from jax.sharding import PartitionSpec as P

LIVE = 4


def compact_matrix(slot_counts, live_rows, capacity):
    sources = slot_counts.shape[0]
    within_slot = jnp.tile(jnp.arange(capacity, dtype=jnp.int32), sources)
    count_slot = jnp.repeat(slot_counts, capacity)
    offsets = jnp.repeat(jnp.cumsum(slot_counts) - slot_counts, capacity)
    target = offsets + within_slot
    alive = within_slot < count_slot
    row_index = jnp.arange(live_rows, dtype=jnp.int32)[:, None]
    return ((row_index == target[None, :]) & alive[None, :]).astype(jnp.bfloat16)


def contract(left, right, left_dim, right_dim):
    return lax.dot_general(
        left, right, (((left_dim,), (right_dim,)), ((), ())), preferred_element_type=jnp.float32
    )


def body(x_rows, cot_rows, counts, w_gate, w_up, w_down, kept_blocks, block_rank):
    expert_count = x_rows.shape[2]
    capacity = x_rows.shape[3]
    model_width = x_rows.shape[4]
    slot_rows = x_rows.reshape(expert_count, capacity, model_width)
    slot_cots = cot_rows.reshape(expert_count, capacity, model_width)
    my_expert = lax.axis_index("expert")
    picked = jnp.arange(expert_count, dtype=jnp.int32)[None, :] == my_expert
    own_counts = jnp.sum(jnp.where(picked, counts[:, 0, :], 0), axis=1)
    chooser = compact_matrix(own_counts, LIVE, capacity)

    def pack_rows(received):
        flat_rows = received.reshape(-1, model_width)
        return jnp.dot(chooser, flat_rows, preferred_element_type=jnp.float32).astype(jnp.bfloat16)

    got_rows, got_cots = (
        lax.all_to_all(slot_rows, "expert", split_axis=0, concat_axis=0, tiled=True),
        lax.all_to_all(slot_cots, "expert", split_axis=0, concat_axis=0, tiled=True),
    )
    group_rows, group_cots = (
        lax.all_gather(pack_rows(got_rows), "dp", axis=0, tiled=True),
        lax.all_gather(pack_rows(got_cots), "dp", axis=0, tiled=True),
    )
    gate_weight = w_gate[0]
    up_weight = w_up[0]
    down_weight = w_down[0]
    keep_mask = (block_rank.reshape(()) < kept_blocks.reshape(())).astype(jnp.float32)
    gate_pre = jnp.dot(group_rows, gate_weight, preferred_element_type=jnp.float32)
    up_pre = jnp.dot(group_rows, up_weight, preferred_element_type=jnp.float32)
    sigmoid_gate = jax.nn.sigmoid(gate_pre)
    activated = gate_pre * sigmoid_gate
    hidden = (activated * up_pre * keep_mask).astype(jnp.bfloat16)
    hidden_grad = contract(group_cots, down_weight, 1, 1)
    up_grad = (hidden_grad * activated * keep_mask).astype(jnp.bfloat16)
    gate_grad = (
        hidden_grad * up_pre * sigmoid_gate * (1.0 + gate_pre * (1.0 - sigmoid_gate)) * keep_mask
    ).astype(jnp.bfloat16)
    grad_down = contract(hidden, group_cots, 0, 0).astype(jnp.bfloat16)
    grad_gate = contract(group_rows, gate_grad, 0, 0).astype(jnp.bfloat16)
    grad_up = contract(group_rows, up_grad, 0, 0).astype(jnp.bfloat16)
    whole_term = contract(gate_grad, gate_weight, 1, 1) + contract(up_grad, up_weight, 1, 1)
    row_grads = lax.psum_scatter(whole_term, "dp", scatter_dimension=0, tiled=True)
    row_grads = row_grads.astype(jnp.bfloat16)
    slot_grads = contract(chooser, row_grads, 0, 0).astype(jnp.bfloat16)
    slot_grads = slot_grads.reshape(expert_count, capacity, model_width)
    returned = lax.all_to_all(slot_grads, "expert", split_axis=0, concat_axis=0, tiled=True)
    grad_rows = returned.reshape(1, 1, expert_count, capacity, model_width)
    return (grad_rows, grad_gate[None], grad_up[None], grad_down[None])


def exchange_kernel(
    x_ref, cot_ref, counts_hbm, kept_ref, rank_ref, wg_ref, wu_ref, wd_ref,
    final_out, gate_out, up_out, down_out,
    slots, counts_ref,
    stage, landed, rows, w_in, w_down, acc_gu, acc_dh, sib_out, sib_in, part, regroup, unit, unit_in,
    s1_send, s1_recv, z_send, z_recv, y_send, y_recv, sb_send, sb_recv,
    r1_send, r1_recv, r2_send, r2_recv, load_sem, slot_sem,
):
    s = lax.axis_index("expert")
    d = lax.axis_index("dp")
    z, y, c = d // 4, (d // 2) % 2, d % 2
    width = rows.shape[1]
    half = width // 2
    quarter = half // 4
    pair = half // 2

    def device(e, zz, yy, cc):
        return (e, zz * 4 + yy * 2 + cc)

    def remote(src, dst, send, recv, where):
        return pltpu.make_async_remote_copy(
            src_ref=src, dst_ref=dst, send_sem=send, recv_sem=recv, device_id=where,
            device_id_type=pl.DeviceIdType.MESH,
        )

    near = [(0, 1), (1, 0), (1, 1)]
    others = [(de, dz, dy) for dz in (2, 3, 1, 0) for de in (1, 0) for dy in (1, 0) if (de, dz, dy) != (0, 0, 0)]

    def near_device(de, dc):
        return device((s + de) % 2, z, y, (c + dc) % 2)

    def other_device(de, dz, dy):
        return device((s + de) % 2, (z + dz) % 4, (y + dy) % 2, c)

    slot_loads = [
        pltpu.make_async_copy(x_ref.at[0, 0], slots.at[0], slot_sem.at[0]),
        pltpu.make_async_copy(cot_ref.at[0, 0], slots.at[1], slot_sem.at[1]),
        pltpu.make_async_copy(counts_hbm, counts_ref, slot_sem.at[2]),
    ]
    loads = [
        pltpu.make_async_copy(wg_ref.at[0], w_in.at[:, pl.ds(0, 128)], load_sem.at[0]),
        pltpu.make_async_copy(wu_ref.at[0], w_in.at[:, pl.ds(128, 128)], load_sem.at[1]),
        pltpu.make_async_copy(wd_ref.at[0], w_down, load_sem.at[2]),
    ]
    barrier = pltpu.get_barrier_semaphore()
    greeted = [near_device(0, 1), near_device(1, 1)] + [other_device(*other) for other in others]
    for where in greeted:
        pl.semaphore_signal(barrier, inc=1, device_id=where, device_id_type=pl.DeviceIdType.MESH)
    for load in slot_loads + loads:
        load.start()
    for load in slot_loads:
        load.wait()

    row16 = lax.broadcasted_iota(jnp.int32, (16, quarter), 0)
    slot = (row16 >> 2) & 1
    for e in range(2):
        live = jnp.where(s == 0, counts_ref[0, 0, e], counts_ref[1, 0, e])
        sources = [slots[0, e].astype(jnp.float32), slots[1, e].astype(jnp.float32)]
        for h in range(2):
            value = jnp.zeros((16, quarter), jnp.float32)
            for r in range(16):
                t, k, g = r // 8, (r // 4) % 2, r % 4
                start = h * half + g * quarter
                line = sources[t][k:k + 1, start:start + quarter]
                value = jnp.where(row16 == r, jnp.broadcast_to(line, value.shape), value)
            stage[e, h] = jnp.where(slot < live, value, 0.0).astype(jnp.bfloat16)

    i = lax.broadcasted_iota(jnp.int32, (64, 64), 0)
    j = lax.broadcasted_iota(jnp.int32, (64, 64), 1)
    order = (
        ((i >> 4) == (j & 3))
        & (((i >> 3) & 1) == ((j >> 3) & 1))
        & (((i >> 2) & 1) == ((j >> 5) & 1))
        & (((i >> 1) & 1) == ((j >> 4) & 1))
        & ((i & 1) == ((j >> 2) & 1))
    ).astype(jnp.float32).astype(jnp.bfloat16)

    pl.semaphore_wait(barrier, len(greeted))

    mine = pl.ds(pl.multiple_of((c * 2 + s) * 16, 16), 16)
    sends = []
    first = []
    for de, dc in near:
        index = de * 2 + dc
        copy = remote(
            stage.at[(s + de) % 2, (c + dc) % 2], landed.at[mine, :], s1_send.at[index], s1_recv.at[index],
            near_device(de, dc),
        )
        copy.start()
        first.append(copy)
    landed[mine, :] = stage[s, c]
    for copy in first:
        copy.wait_recv()
    sends += first

    def block(zz, yy, hh):
        return rows.at[
            pl.ds(pl.multiple_of((yy * 4 + zz) * 16, 16), 16), pl.ds(pl.multiple_of(hh * half, 128), half)
        ]

    ordered = jnp.dot(order, landed[...], preferred_element_type=jnp.float32).astype(jnp.bfloat16)
    my_rows = pl.ds(pl.multiple_of((y * 4 + z) * 16, 16), 16)
    for g in range(4):
        rows[my_rows, pl.ds(pl.multiple_of(c * half + g * quarter, 128), quarter)] = ordered[g * 16:(g + 1) * 16, :]

    def forward(ref, send, recv, where):
        copy = remote(ref, ref, send, recv, where)
        copy.start()
        sends.append(copy)
        return copy

    sibling = device(s, z, y, 1 - c)
    opposite = device(s, z, 1 - y, c)
    own = block(z, y, c)
    z_copies = {}
    for dz in (2, 1, 3):
        z_copies[dz] = forward(own, z_send.at[dz - 1], z_recv.at[dz - 1], device(s, (z + dz) % 4, y, c))
    y_copies = [forward(own, y_send.at[0], y_recv.at[0], opposite)]
    s_copies = [forward(own, sb_send.at[0], sb_recv.at[0], sibling)]
    for dz in (1, 3, 2):
        z_copies[dz].wait_recv()
        got = block((z + 4 - dz) % 4, y, c)
        y_copies.append(forward(got, y_send.at[dz], y_recv.at[dz], opposite))
        s_copies.append(forward(got, sb_send.at[dz], sb_recv.at[dz], sibling))

    for load in loads:
        load.wait()

    def forward_part(yy, hh, start):
        columns = pl.ds(pl.multiple_of(hh * half, 256), half)
        some = rows[pl.ds(pl.multiple_of(yy * 64, 64), 64), columns]
        both = jnp.dot(some, w_in[columns, :], preferred_element_type=jnp.float32)
        back = lax.dot_general(
            some, w_down[:, columns], (((1,), (1,)), ((), ())), preferred_element_type=jnp.float32
        )
        both = both.reshape(4, 16, 256)[:, 0:8].reshape(32, 256)
        back = back.reshape(4, 16, 128)[:, 8:16].reshape(32, 128)
        place = pl.ds(pl.multiple_of(yy * 32, 32), 32)
        if not start:
            both = both + acc_gu[place, :]
            back = back + acc_dh[place, :]
        acc_gu[place, :] = both
        acc_dh[place, :] = back

    last = []

    def pass_on(n, dz):
        y_copies[n].wait_recv()
        got = block((z + 4 - dz) % 4, 1 - y, c)
        last.append(forward(got, sb_send.at[4 + dz], sb_recv.at[4 + dz], sibling))

    forward_part(y, c, True)
    pass_on(0, 0)
    for copy in s_copies:
        copy.wait_recv()
    forward_part(y, 1 - c, False)
    for n, dz in ((1, 1), (2, 3), (3, 2)):
        pass_on(n, dz)
    forward_part(1 - y, c, True)
    for copy in last:
        copy.wait_recv()
    forward_part(1 - y, 1 - c, False)

    keep = jnp.where(rank_ref[0, 0] < kept_ref[0], 1.0, 0.0).astype(jnp.float32)
    gate_pre = acc_gu[:, 0:128]
    up_pre = acc_gu[:, 128:256]
    hidden_grad = acc_dh[...]
    sigmoid_gate = jax.nn.sigmoid(gate_pre)
    activated = gate_pre * sigmoid_gate
    hidden = activated * up_pre * keep
    up_grad = hidden_grad * activated * keep
    gate_grad = hidden_grad * up_pre * sigmoid_gate * (1.0 + gate_pre * (1.0 - sigmoid_gate)) * keep
    both_grad = jnp.concatenate([gate_grad, up_grad], axis=1)
    both_bf16 = both_grad.astype(jnp.bfloat16)

    si = lax.broadcasted_iota(jnp.int32, (64, 64), 0)
    sj = lax.broadcasted_iota(jnp.int32, (64, 64), 1)
    split = (
        ((sj >> 3) == ((si & 31) >> 2))
        & ((sj & 3) == (si & 3))
        & (((sj >> 2) & 1) == jnp.where(si >= 32, c, 1 - c))
    ).astype(jnp.float32).astype(jnp.bfloat16)
    by_core = jnp.dot(split, both_bf16, preferred_element_type=jnp.float32).astype(jnp.bfloat16)
    sib_copies = []
    for n in range(4):
        term = lax.dot_general(
            by_core, w_in[n * pair:(n + 1) * pair, :], (((1,), (1,)), ((), ())), preferred_element_type=jnp.float32
        )
        sib_out[n] = term[0:32].astype(jnp.bfloat16)
        copy = remote(sib_out.at[n], sib_in.at[n], r1_send.at[n], r1_recv.at[n], sibling)
        copy.start()
        sib_copies.append(copy)
        part[n] = term[32:64]
    sends += sib_copies

    zeros = jnp.zeros((8, 8, 128), jnp.float32)
    hidden_pad = jnp.concatenate([zeros, hidden.reshape(8, 8, 128)], axis=1).reshape(128, 128).astype(jnp.bfloat16)
    zeros2 = jnp.zeros((8, 8, 256), jnp.float32)
    both_pad = jnp.concatenate([both_grad.reshape(8, 8, 256), zeros2], axis=1).reshape(128, 256).astype(jnp.bfloat16)

    ui = lax.broadcasted_iota(jnp.int32, (256, 256), 0)
    uj = lax.broadcasted_iota(jnp.int32, (256, 256), 1)
    spread = (
        ((uj >> 5) == ((ui >> 1) & 7))
        & ((uj & 1) == (ui & 1))
        & (((uj >> 1) & 1) == ((ui >> 4) & 1))
        & (((uj >> 2) & 7) == (ui >> 5))
    ).astype(jnp.float32).astype(jnp.bfloat16)
    for n in range(4):
        sib_copies[n].wait_recv()
        total = (part[n] + sib_in[n].astype(jnp.float32)).astype(jnp.bfloat16)
        regroup[n * 64:n * 64 + 32, :] = total[:, 0:quarter]
        regroup[n * 64 + 32:n * 64 + 64, :] = total[:, quarter:]
    unit[...] = jnp.dot(spread, regroup[...], preferred_element_type=jnp.float32).astype(jnp.bfloat16)

    def unit_of(ee, zz, yy):
        return unit.at[pl.ds(pl.multiple_of(((yy * 4 + zz) * 2 + ee) * 16, 16), 16), :]

    unit_copies = []
    for de, dz, dy in others:
        index = de * 8 + dz * 2 + dy
        copy = remote(
            unit_of((s + de) % 2, (z + dz) % 4, (y + dy) % 2), unit_in.at[index],
            r2_send.at[index], r2_recv.at[index], other_device(de, dz, dy),
        )
        copy.start()
        unit_copies.append(copy)
    sends += unit_copies

    for n in range(4):
        columns = pl.ds(n * pair, pair)
        some = rows[:, columns]
        down_out[0, :, columns] = lax.dot_general(
            hidden_pad, some, (((0,), (0,)), ((), ())), preferred_element_type=jnp.float32
        ).astype(jnp.bfloat16)
        inner = lax.dot_general(
            some, both_pad, (((0,), (0,)), ((), ())), preferred_element_type=jnp.float32
        ).astype(jnp.bfloat16)
        gate_out[0, columns, :] = inner[:, 0:128]
        up_out[0, columns, :] = inner[:, 128:256]

    for copy in unit_copies:
        copy.wait_recv()
    for de in range(2):
        if de == 0:
            result = unit[pl.ds(pl.multiple_of(((y * 4 + z) * 2 + s) * 16, 16), 16), :].astype(jnp.float32)
        else:
            result = unit_in[8].astype(jnp.float32)
        for index in range(1, 8):
            result = result + unit_in[de * 8 + index].astype(jnp.float32)
        final_out[pl.ds(pl.multiple_of(((s + de) % 2) * 16, 16), 16), :] = result.astype(jnp.bfloat16)
    for copy in sends:
        copy.wait_send()


def finish_kernel(final_ref, gate_ref, up_ref, down_ref, rows_out, gate_out, up_out, down_out, lines, sem, line_sem):
    copies = []
    depth = gate_ref.shape[1] // 4
    lanes = down_ref.shape[1] // 4
    for n in range(4):
        some = pl.ds(n * depth, depth)
        few = pl.ds(n * lanes, lanes)
        copies += [
            pltpu.make_async_copy(gate_ref.at[:, some, :], gate_out.at[:, some, :], sem.at[n]),
            pltpu.make_async_copy(up_ref.at[:, some, :], up_out.at[:, some, :], sem.at[4 + n]),
            pltpu.make_async_copy(down_ref.at[:, few, :], down_out.at[:, few, :], sem.at[8 + n]),
        ]
    for copy in copies:
        copy.start()
    quarter = final_ref.shape[1]
    final = final_ref[...].astype(jnp.float32)
    for e in range(2):
        for g in range(8):
            start = e * 16 + g * 2
            lines[0, 0, e, :, g * quarter:(g + 1) * quarter] = final[start:start + 2, :].astype(jnp.bfloat16)
    line_copy = pltpu.make_async_copy(lines, rows_out, line_sem)
    line_copy.start()
    for copy in copies:
        copy.wait()
    line_copy.wait()


def kernel_body(x_rows, cot_rows, counts, w_gate, w_up, w_down, kept_blocks, block_rank):
    width = x_rows.shape[4]
    quarter = width // 8
    pair = width // 4

    vmem = pl.BlockSpec(memory_space=pltpu.VMEM)
    hbm = pl.BlockSpec(memory_space=pltpu.HBM)
    anywhere = pl.BlockSpec(memory_space=pl.ANY)
    smem = pl.BlockSpec(memory_space=pltpu.SMEM)
    held = [
        pltpu.with_memory_space_constraint(a, pltpu.HBM) for a in (x_rows, cot_rows, counts, w_gate, w_up, w_down)
    ]
    bf16, f32 = jnp.bfloat16, jnp.float32
    dma = pltpu.SemaphoreType.DMA
    final_rows, grad_gate, grad_up, grad_down = pl.pallas_call(
        exchange_kernel,
        out_shape=(
            jax.ShapeDtypeStruct((32, quarter), bf16),
            jax.ShapeDtypeStruct(w_gate.shape, bf16),
            jax.ShapeDtypeStruct(w_up.shape, bf16),
            jax.ShapeDtypeStruct(w_down.shape, bf16),
        ),
        in_specs=[hbm, hbm, hbm, smem, smem, hbm, hbm, hbm],
        out_specs=(vmem, vmem, vmem, vmem),
        scratch_shapes=[
            pltpu.VMEM((2,) + x_rows.shape[2:], bf16),
            pltpu.SMEM(counts.shape, jnp.int32),
            pltpu.VMEM((2, 2, 16, quarter), bf16),
            pltpu.VMEM((64, quarter), bf16),
            pltpu.VMEM((128, width), bf16),
            pltpu.VMEM((width, 256), bf16),
            pltpu.VMEM((128, width), bf16),
            pltpu.VMEM((64, 256), f32),
            pltpu.VMEM((64, 128), f32),
            pltpu.VMEM((4, 32, pair), bf16),
            pltpu.VMEM((4, 32, pair), bf16),
            pltpu.VMEM((4, 32, pair), f32),
            pltpu.VMEM((256, quarter), bf16),
            pltpu.VMEM((256, quarter), bf16),
            pltpu.VMEM((16, 16, quarter), bf16),
            dma((4,)), dma((4,)), dma((3,)), dma((3,)), dma((4,)), dma((4,)), dma((8,)), dma((8,)),
            dma((4,)), dma((4,)), dma((16,)), dma((16,)), dma((3,)), dma((3,)),
        ],
        compiler_params=pltpu.CompilerParams(
            collective_id=0, has_side_effects=True, vmem_limit_bytes=32 * 1024 * 1024
        ),
        name="expert_backward",
    )(*held[:3], kept_blocks, block_rank, *held[3:])
    return pl.pallas_call(
        finish_kernel,
        out_shape=tuple(jax.ShapeDtypeStruct(a.shape, bf16) for a in (x_rows, w_gate, w_up, w_down)),
        in_specs=[vmem, anywhere, anywhere, anywhere],
        out_specs=(anywhere, anywhere, anywhere, anywhere),
        scratch_shapes=[pltpu.VMEM(x_rows.shape, bf16), dma((12,)), dma(())],
        compiler_params=pltpu.CompilerParams(vmem_limit_bytes=16 * 1024 * 1024),
        name="write_outputs",
    )(final_rows, grad_gate, grad_up, grad_down)


def solution(mesh):
    in_specs = (
        P("expert", "dp", None, None, None),
        P("expert", "dp", None, None, None),
        P(None, "dp", None),
        P("expert", None, "dp"),
        P("expert", None, "dp"),
        P("expert", "dp", None),
        P("expert"),
        P("expert", "dp"),
    )
    out_specs = (
        P("expert", "dp", None, None, None),
        P("expert", None, "dp"),
        P("expert", None, "dp"),
        P("expert", "dp", None),
    )
    small = mesh.shape["expert"] == 2 and mesh.shape["dp"] == 16
    return jax.shard_map(kernel_body if small else body, mesh=mesh, in_specs=in_specs, out_specs=out_specs, check_vma=False)
```

```python
import jax
import jax.numpy as jnp
from jax import lax
from jax.experimental import pallas as pl
from jax.experimental.pallas import tpu as pltpu
from jax.sharding import PartitionSpec as P

LIVE = 4


def compact_matrix(slot_counts, live_rows, capacity):
    sources = slot_counts.shape[0]
    within_slot = jnp.tile(jnp.arange(capacity, dtype=jnp.int32), sources)
    count_slot = jnp.repeat(slot_counts, capacity)
    offsets = jnp.repeat(jnp.cumsum(slot_counts) - slot_counts, capacity)
    target = offsets + within_slot
    alive = within_slot < count_slot
    row_index = jnp.arange(live_rows, dtype=jnp.int32)[:, None]
    return ((row_index == target[None, :]) & alive[None, :]).astype(jnp.bfloat16)


def contract(left, right, left_dim, right_dim):
    return lax.dot_general(
        left, right, (((left_dim,), (right_dim,)), ((), ())), preferred_element_type=jnp.float32
    )


def body(x_rows, cot_rows, counts, w_gate, w_up, w_down, kept_blocks, block_rank):
    expert_count = x_rows.shape[2]
    capacity = x_rows.shape[3]
    model_width = x_rows.shape[4]
    slot_rows = x_rows.reshape(expert_count, capacity, model_width)
    slot_cots = cot_rows.reshape(expert_count, capacity, model_width)
    my_expert = lax.axis_index("expert")
    picked = jnp.arange(expert_count, dtype=jnp.int32)[None, :] == my_expert
    own_counts = jnp.sum(jnp.where(picked, counts[:, 0, :], 0), axis=1)
    chooser = compact_matrix(own_counts, LIVE, capacity)

    def pack_rows(received):
        flat_rows = received.reshape(-1, model_width)
        return jnp.dot(chooser, flat_rows, preferred_element_type=jnp.float32).astype(jnp.bfloat16)

    got_rows, got_cots = (
        lax.all_to_all(slot_rows, "expert", split_axis=0, concat_axis=0, tiled=True),
        lax.all_to_all(slot_cots, "expert", split_axis=0, concat_axis=0, tiled=True),
    )
    group_rows, group_cots = (
        lax.all_gather(pack_rows(got_rows), "dp", axis=0, tiled=True),
        lax.all_gather(pack_rows(got_cots), "dp", axis=0, tiled=True),
    )
    gate_weight = w_gate[0]
    up_weight = w_up[0]
    down_weight = w_down[0]
    keep_mask = (block_rank.reshape(()) < kept_blocks.reshape(())).astype(jnp.float32)
    gate_pre = jnp.dot(group_rows, gate_weight, preferred_element_type=jnp.float32)
    up_pre = jnp.dot(group_rows, up_weight, preferred_element_type=jnp.float32)
    sigmoid_gate = jax.nn.sigmoid(gate_pre)
    activated = gate_pre * sigmoid_gate
    hidden = (activated * up_pre * keep_mask).astype(jnp.bfloat16)
    hidden_grad = contract(group_cots, down_weight, 1, 1)
    up_grad = (hidden_grad * activated * keep_mask).astype(jnp.bfloat16)
    gate_grad = (
        hidden_grad * up_pre * sigmoid_gate * (1.0 + gate_pre * (1.0 - sigmoid_gate)) * keep_mask
    ).astype(jnp.bfloat16)
    grad_down = contract(hidden, group_cots, 0, 0).astype(jnp.bfloat16)
    grad_gate = contract(group_rows, gate_grad, 0, 0).astype(jnp.bfloat16)
    grad_up = contract(group_rows, up_grad, 0, 0).astype(jnp.bfloat16)
    whole_term = contract(gate_grad, gate_weight, 1, 1) + contract(up_grad, up_weight, 1, 1)
    row_grads = lax.psum_scatter(whole_term, "dp", scatter_dimension=0, tiled=True)
    row_grads = row_grads.astype(jnp.bfloat16)
    slot_grads = contract(chooser, row_grads, 0, 0).astype(jnp.bfloat16)
    slot_grads = slot_grads.reshape(expert_count, capacity, model_width)
    returned = lax.all_to_all(slot_grads, "expert", split_axis=0, concat_axis=0, tiled=True)
    grad_rows = returned.reshape(1, 1, expert_count, capacity, model_width)
    return (grad_rows, grad_gate[None], grad_up[None], grad_down[None])


def exchange_kernel(
    x_ref, cot_ref, counts_hbm, kept_ref, rank_ref, wg_ref, wu_ref, wd_ref,
    final_out, gate_out, up_out, down_out,
    slots, counts_ref,
    stage, pieces, rows, w_in, w_down, acc_gu, acc_dh, sib_out, sib_in, part, regroup, unit, unit_in,
    z_send, z_recv, y_send, y_recv, sb_send, sb_recv,
    r1_send, r1_recv, r2_send, r2_recv, load_sem, slot_sem,
):
    s = lax.axis_index("expert")
    d = lax.axis_index("dp")
    z, y, c = d // 4, (d // 2) % 2, d % 2
    width = rows.shape[1]
    half = width // 2
    quarter = half // 4
    pair = half // 2

    def device(e, zz, yy, cc):
        return (e, zz * 4 + yy * 2 + cc)

    def remote(src, dst, send, recv, where):
        return pltpu.make_async_remote_copy(
            src_ref=src, dst_ref=dst, send_sem=send, recv_sem=recv, device_id=where,
            device_id_type=pl.DeviceIdType.MESH,
        )

    others = [(de, dz, dy) for dz in (2, 3, 1, 0) for de in (1, 0) for dy in (1, 0) if (de, dz, dy) != (0, 0, 0)]

    def other_device(de, dz, dy):
        return device((s + de) % 2, (z + dz) % 4, (y + dy) % 2, c)

    slot_loads = [
        pltpu.make_async_copy(x_ref.at[0, 0], slots.at[0], slot_sem.at[0]),
        pltpu.make_async_copy(cot_ref.at[0, 0], slots.at[1], slot_sem.at[1]),
        pltpu.make_async_copy(counts_hbm, counts_ref, slot_sem.at[2]),
    ]
    loads = [
        pltpu.make_async_copy(wg_ref.at[0], w_in.at[:, pl.ds(0, 128)], load_sem.at[0]),
        pltpu.make_async_copy(wu_ref.at[0], w_in.at[:, pl.ds(128, 128)], load_sem.at[1]),
        pltpu.make_async_copy(wd_ref.at[0], w_down, load_sem.at[2]),
    ]
    barrier = pltpu.get_barrier_semaphore()
    greeted = [device(s, z, y, 1 - c)] + [other_device(*other) for other in others]
    for where in greeted:
        pl.semaphore_signal(barrier, inc=1, device_id=where, device_id_type=pl.DeviceIdType.MESH)
    for load in slot_loads + loads:
        load.start()
    for load in slot_loads:
        load.wait()

    row8 = lax.broadcasted_iota(jnp.int32, (8, quarter), 0)
    for e in range(2):
        live = jnp.where(s == 0, counts_ref[0, 0, e], counts_ref[1, 0, e])
        for t in range(2):
            source = slots[t, e].astype(jnp.float32)
            groups = []
            for k in range(2):
                value = jnp.zeros((8, quarter), jnp.float32)
                for g in range(8):
                    line = source[k:k + 1, g * quarter:(g + 1) * quarter]
                    value = jnp.where(row8 == g, jnp.broadcast_to(line, value.shape), value)
                groups.append(value * jnp.where(k < live, 1.0, 0.0).astype(jnp.float32))
            stage[e, t * 16:(t + 1) * 16, :] = jnp.concatenate(groups, axis=0).astype(jnp.bfloat16)

    i = lax.broadcasted_iota(jnp.int32, (256, 256), 0)
    j = lax.broadcasted_iota(jnp.int32, (256, 256), 1)
    order = (
        ((i >> 5) == (j & 7))
        & (((i >> 4) & 1) == ((j >> 4) & 1))
        & (((i >> 2) & 3) == (j >> 6))
        & (((i >> 1) & 1) == ((j >> 5) & 1))
        & ((i & 1) == ((j >> 3) & 1))
    ).astype(jnp.float32).astype(jnp.bfloat16)

    pl.semaphore_wait(barrier, len(greeted))

    sends = []

    def piece(ss, zz, yy, cc):
        return pieces.at[yy * 2 + cc, pl.ds(pl.multiple_of((zz * 2 + ss) * 32, 32), 32), :]

    line = [(1, 0), (0, 1), (1, 1), (0, 3), (1, 3), (0, 2), (1, 2)]
    z_copies = {}
    for de, dz in reversed(line):
        index = de * 4 + dz
        copy = remote(
            stage.at[(s + de) % 2], piece(s, z, y, c), z_send.at[index], z_recv.at[index], other_device(de, dz, 0)
        )
        copy.start()
        z_copies[de, dz] = copy
        sends.append(copy)
    pieces[y * 2 + c, pl.ds(pl.multiple_of((z * 2 + s) * 32, 32), 32), :] = stage[s]

    def forward(ref, send, recv, where):
        copy = remote(ref, ref, send, recv, where)
        copy.start()
        sends.append(copy)
        return copy

    sibling = device(s, z, y, 1 - c)
    opposite = device(s, z, 1 - y, c)
    y_copies, s_copies = [], []
    for de, dz in [(0, 0)] + line:
        if (de, dz) != (0, 0):
            z_copies[de, dz].wait_recv()
        index = de * 4 + dz
        got = piece((s + de) % 2, (z + 4 - dz) % 4, y, c)
        y_copies.append(forward(got, y_send.at[index], y_recv.at[index], opposite))
        s_copies.append(forward(got, sb_send.at[index], sb_recv.at[index], sibling))

    for load in loads:
        load.wait()

    def arrange(yy, cc):
        ordered = jnp.dot(order, pieces[yy * 2 + cc], preferred_element_type=jnp.float32).astype(jnp.bfloat16)
        place = pl.ds(pl.multiple_of((yy * 2 + cc) * 32, 32), 32)
        for g in range(8):
            rows[place, g * quarter:(g + 1) * quarter] = ordered[g * 32:(g + 1) * 32, :]

    def forward_part(yy, start, stop):
        some = rows[pl.ds(pl.multiple_of(yy * 64, 64), 64), start:stop]
        both = jnp.dot(some, w_in[start:stop, :], preferred_element_type=jnp.float32)
        back = lax.dot_general(
            some, w_down[:, start:stop], (((1,), (1,)), ((), ())), preferred_element_type=jnp.float32
        )
        both = both.reshape(2, 32, 256)[:, 0:16].reshape(32, 256)
        back = back.reshape(2, 32, 128)[:, 16:32].reshape(32, 128)
        place = pl.ds(pl.multiple_of(yy * 32, 32), 32)
        if start > 0:
            both = both + acc_gu[place, :]
            back = back + acc_dh[place, :]
        acc_gu[place, :] = both
        acc_dh[place, :] = back

    last = []

    def pass_on(n):
        y_copies[n].wait_recv()
        de, dz = ([(0, 0)] + line)[n]
        got = piece((s + de) % 2, (z + 4 - dz) % 4, 1 - y, c)
        index = 8 + de * 4 + dz
        last.append(forward(got, sb_send.at[index], sb_recv.at[index], sibling))

    arrange(y, c)
    for n in range(4):
        pass_on(n)
    for copy in s_copies:
        copy.wait_recv()
    arrange(y, 1 - c)
    forward_part(y, 0, half)
    for n in range(4, 8):
        pass_on(n)
    arrange(1 - y, c)
    forward_part(y, half, width)
    for copy in last:
        copy.wait_recv()
    arrange(1 - y, 1 - c)
    forward_part(1 - y, 0, width)

    keep = jnp.where(rank_ref[0, 0] < kept_ref[0], 1.0, 0.0).astype(jnp.float32)
    gate_pre = acc_gu[:, 0:128]
    up_pre = acc_gu[:, 128:256]
    hidden_grad = acc_dh[...]
    sigmoid_gate = jax.nn.sigmoid(gate_pre)
    activated = gate_pre * sigmoid_gate
    hidden = activated * up_pre * keep
    up_grad = hidden_grad * activated * keep
    gate_grad = hidden_grad * up_pre * sigmoid_gate * (1.0 + gate_pre * (1.0 - sigmoid_gate)) * keep
    both_grad = jnp.concatenate([gate_grad, up_grad], axis=1)
    both_bf16 = both_grad.astype(jnp.bfloat16)

    si = lax.broadcasted_iota(jnp.int32, (64, 64), 0)
    sj = lax.broadcasted_iota(jnp.int32, (64, 64), 1)
    split = (
        ((sj >> 5) == ((si & 31) >> 4))
        & ((sj & 15) == (si & 15))
        & (((sj >> 4) & 1) == jnp.where(si >= 32, c, 1 - c))
    ).astype(jnp.float32).astype(jnp.bfloat16)
    by_core = jnp.dot(split, both_bf16, preferred_element_type=jnp.float32).astype(jnp.bfloat16)
    sib_copies = []
    for n in range(4):
        term = lax.dot_general(
            by_core, w_in[n * pair:(n + 1) * pair, :], (((1,), (1,)), ((), ())), preferred_element_type=jnp.float32
        )
        sib_out[n] = term[0:32].astype(jnp.bfloat16)
        copy = remote(sib_out.at[n], sib_in.at[n], r1_send.at[n], r1_recv.at[n], sibling)
        copy.start()
        sib_copies.append(copy)
        part[n] = term[32:64]
    sends += sib_copies

    zeros = jnp.zeros((4, 16, 128), jnp.float32)
    hidden_pad = jnp.concatenate([zeros, hidden.reshape(4, 16, 128)], axis=1).reshape(128, 128).astype(jnp.bfloat16)
    zeros2 = jnp.zeros((4, 16, 256), jnp.float32)
    both_pad = jnp.concatenate([both_grad.reshape(4, 16, 256), zeros2], axis=1).reshape(128, 256).astype(jnp.bfloat16)

    ui = lax.broadcasted_iota(jnp.int32, (256, 256), 0)
    uj = lax.broadcasted_iota(jnp.int32, (256, 256), 1)
    spread = (
        ((uj >> 5) == ((ui >> 1) & 7))
        & ((uj & 1) == (ui & 1))
        & (((uj >> 1) & 1) == ((ui >> 4) & 1))
        & (((uj >> 2) & 7) == (ui >> 5))
    ).astype(jnp.float32).astype(jnp.bfloat16)
    for n in range(4):
        sib_copies[n].wait_recv()
        total = (part[n] + sib_in[n].astype(jnp.float32)).astype(jnp.bfloat16)
        regroup[n * 64:n * 64 + 32, :] = total[:, 0:quarter]
        regroup[n * 64 + 32:n * 64 + 64, :] = total[:, quarter:]
    unit[...] = jnp.dot(spread, regroup[...], preferred_element_type=jnp.float32).astype(jnp.bfloat16)

    def unit_of(ee, zz, yy):
        return unit.at[pl.ds(pl.multiple_of(((yy * 4 + zz) * 2 + ee) * 16, 16), 16), :]

    unit_copies = []
    for de, dz, dy in others:
        index = de * 8 + dz * 2 + dy
        copy = remote(
            unit_of((s + de) % 2, (z + dz) % 4, (y + dy) % 2), unit_in.at[index],
            r2_send.at[index], r2_recv.at[index], other_device(de, dz, dy),
        )
        copy.start()
        unit_copies.append(copy)
    sends += unit_copies

    for n in range(4):
        columns = pl.ds(n * pair, pair)
        some = rows[:, columns]
        down_out[0, :, columns] = lax.dot_general(
            hidden_pad, some, (((0,), (0,)), ((), ())), preferred_element_type=jnp.float32
        ).astype(jnp.bfloat16)
        inner = lax.dot_general(
            some, both_pad, (((0,), (0,)), ((), ())), preferred_element_type=jnp.float32
        ).astype(jnp.bfloat16)
        gate_out[0, columns, :] = inner[:, 0:128]
        up_out[0, columns, :] = inner[:, 128:256]

    for copy in unit_copies:
        copy.wait_recv()
    for de in range(2):
        if de == 0:
            result = unit[pl.ds(pl.multiple_of(((y * 4 + z) * 2 + s) * 16, 16), 16), :].astype(jnp.float32)
        else:
            result = unit_in[8].astype(jnp.float32)
        for index in range(1, 8):
            result = result + unit_in[de * 8 + index].astype(jnp.float32)
        final_out[pl.ds(pl.multiple_of(((s + de) % 2) * 16, 16), 16), :] = result.astype(jnp.bfloat16)
    for copy in sends:
        copy.wait_send()


def finish_kernel(final_ref, gate_ref, up_ref, down_ref, rows_out, gate_out, up_out, down_out, lines, sem, line_sem):
    copies = []
    depth = gate_ref.shape[1] // 4
    lanes = down_ref.shape[1] // 4
    for n in range(4):
        some = pl.ds(n * depth, depth)
        few = pl.ds(n * lanes, lanes)
        copies += [
            pltpu.make_async_copy(gate_ref.at[:, some, :], gate_out.at[:, some, :], sem.at[n]),
            pltpu.make_async_copy(up_ref.at[:, some, :], up_out.at[:, some, :], sem.at[4 + n]),
            pltpu.make_async_copy(down_ref.at[:, few, :], down_out.at[:, few, :], sem.at[8 + n]),
        ]
    for copy in copies:
        copy.start()
    quarter = final_ref.shape[1]
    final = final_ref[...].astype(jnp.float32)
    for e in range(2):
        for g in range(8):
            start = e * 16 + g * 2
            lines[0, 0, e, :, g * quarter:(g + 1) * quarter] = final[start:start + 2, :].astype(jnp.bfloat16)
    line_copy = pltpu.make_async_copy(lines, rows_out, line_sem)
    line_copy.start()
    for copy in copies:
        copy.wait()
    line_copy.wait()


def kernel_body(x_rows, cot_rows, counts, w_gate, w_up, w_down, kept_blocks, block_rank):
    width = x_rows.shape[4]
    quarter = width // 8
    pair = width // 4

    vmem = pl.BlockSpec(memory_space=pltpu.VMEM)
    hbm = pl.BlockSpec(memory_space=pltpu.HBM)
    anywhere = pl.BlockSpec(memory_space=pl.ANY)
    smem = pl.BlockSpec(memory_space=pltpu.SMEM)
    held = [
        pltpu.with_memory_space_constraint(a, pltpu.HBM) for a in (x_rows, cot_rows, counts, w_gate, w_up, w_down)
    ]
    bf16, f32 = jnp.bfloat16, jnp.float32
    dma = pltpu.SemaphoreType.DMA
    final_rows, grad_gate, grad_up, grad_down = pl.pallas_call(
        exchange_kernel,
        out_shape=(
            jax.ShapeDtypeStruct((32, quarter), bf16),
            jax.ShapeDtypeStruct(w_gate.shape, bf16),
            jax.ShapeDtypeStruct(w_up.shape, bf16),
            jax.ShapeDtypeStruct(w_down.shape, bf16),
        ),
        in_specs=[hbm, hbm, hbm, smem, smem, hbm, hbm, hbm],
        out_specs=(vmem, vmem, vmem, vmem),
        scratch_shapes=[
            pltpu.VMEM((2,) + x_rows.shape[2:], bf16),
            pltpu.SMEM(counts.shape, jnp.int32),
            pltpu.VMEM((2, 32, quarter), bf16),
            pltpu.VMEM((4, 256, quarter), bf16),
            pltpu.VMEM((128, width), bf16),
            pltpu.VMEM((width, 256), bf16),
            pltpu.VMEM((128, width), bf16),
            pltpu.VMEM((64, 256), f32),
            pltpu.VMEM((64, 128), f32),
            pltpu.VMEM((4, 32, pair), bf16),
            pltpu.VMEM((4, 32, pair), bf16),
            pltpu.VMEM((4, 32, pair), f32),
            pltpu.VMEM((256, quarter), bf16),
            pltpu.VMEM((256, quarter), bf16),
            pltpu.VMEM((16, 16, quarter), bf16),
            dma((8,)), dma((8,)), dma((8,)), dma((8,)), dma((16,)), dma((16,)),
            dma((4,)), dma((4,)), dma((16,)), dma((16,)), dma((3,)), dma((3,)),
        ],
        compiler_params=pltpu.CompilerParams(
            collective_id=0, has_side_effects=True, vmem_limit_bytes=32 * 1024 * 1024
        ),
        name="expert_backward",
    )(*held[:3], kept_blocks, block_rank, *held[3:])
    return pl.pallas_call(
        finish_kernel,
        out_shape=tuple(jax.ShapeDtypeStruct(a.shape, bf16) for a in (x_rows, w_gate, w_up, w_down)),
        in_specs=[vmem, anywhere, anywhere, anywhere],
        out_specs=(anywhere, anywhere, anywhere, anywhere),
        scratch_shapes=[pltpu.VMEM(x_rows.shape, bf16), dma((12,)), dma(())],
        compiler_params=pltpu.CompilerParams(vmem_limit_bytes=16 * 1024 * 1024),
        name="write_outputs",
    )(final_rows, grad_gate, grad_up, grad_down)


def solution(mesh):
    in_specs = (
        P("expert", "dp", None, None, None),
        P("expert", "dp", None, None, None),
        P(None, "dp", None),
        P("expert", None, "dp"),
        P("expert", None, "dp"),
        P("expert", "dp", None),
        P("expert"),
        P("expert", "dp"),
    )
    out_specs = (
        P("expert", "dp", None, None, None),
        P("expert", None, "dp"),
        P("expert", None, "dp"),
        P("expert", "dp", None),
    )
    small = mesh.shape["expert"] == 2 and mesh.shape["dp"] == 16
    return jax.shard_map(kernel_body if small else body, mesh=mesh, in_specs=in_specs, out_specs=out_specs, check_vma=False)
```

```python
import jax
import jax.numpy as jnp
from jax import lax
from jax.experimental import pallas as pl
from jax.experimental.pallas import tpu as pltpu
from jax.sharding import PartitionSpec as P

LIVE = 4


def compact_matrix(slot_counts, live_rows, capacity):
    sources = slot_counts.shape[0]
    within_slot = jnp.tile(jnp.arange(capacity, dtype=jnp.int32), sources)
    count_slot = jnp.repeat(slot_counts, capacity)
    offsets = jnp.repeat(jnp.cumsum(slot_counts) - slot_counts, capacity)
    target = offsets + within_slot
    alive = within_slot < count_slot
    row_index = jnp.arange(live_rows, dtype=jnp.int32)[:, None]
    return ((row_index == target[None, :]) & alive[None, :]).astype(jnp.bfloat16)


def contract(left, right, left_dim, right_dim):
    return lax.dot_general(
        left, right, (((left_dim,), (right_dim,)), ((), ())), preferred_element_type=jnp.float32
    )


def body(x_rows, cot_rows, counts, w_gate, w_up, w_down, kept_blocks, block_rank):
    expert_count = x_rows.shape[2]
    capacity = x_rows.shape[3]
    model_width = x_rows.shape[4]
    slot_rows = x_rows.reshape(expert_count, capacity, model_width)
    slot_cots = cot_rows.reshape(expert_count, capacity, model_width)
    my_expert = lax.axis_index("expert")
    picked = jnp.arange(expert_count, dtype=jnp.int32)[None, :] == my_expert
    own_counts = jnp.sum(jnp.where(picked, counts[:, 0, :], 0), axis=1)
    chooser = compact_matrix(own_counts, LIVE, capacity)

    def pack_rows(received):
        flat_rows = received.reshape(-1, model_width)
        return jnp.dot(chooser, flat_rows, preferred_element_type=jnp.float32).astype(jnp.bfloat16)

    got_rows, got_cots = (
        lax.all_to_all(slot_rows, "expert", split_axis=0, concat_axis=0, tiled=True),
        lax.all_to_all(slot_cots, "expert", split_axis=0, concat_axis=0, tiled=True),
    )
    group_rows, group_cots = (
        lax.all_gather(pack_rows(got_rows), "dp", axis=0, tiled=True),
        lax.all_gather(pack_rows(got_cots), "dp", axis=0, tiled=True),
    )
    gate_weight = w_gate[0]
    up_weight = w_up[0]
    down_weight = w_down[0]
    keep_mask = (block_rank.reshape(()) < kept_blocks.reshape(())).astype(jnp.float32)
    gate_pre = jnp.dot(group_rows, gate_weight, preferred_element_type=jnp.float32)
    up_pre = jnp.dot(group_rows, up_weight, preferred_element_type=jnp.float32)
    sigmoid_gate = jax.nn.sigmoid(gate_pre)
    activated = gate_pre * sigmoid_gate
    hidden = (activated * up_pre * keep_mask).astype(jnp.bfloat16)
    hidden_grad = contract(group_cots, down_weight, 1, 1)
    up_grad = (hidden_grad * activated * keep_mask).astype(jnp.bfloat16)
    gate_grad = (
        hidden_grad * up_pre * sigmoid_gate * (1.0 + gate_pre * (1.0 - sigmoid_gate)) * keep_mask
    ).astype(jnp.bfloat16)
    grad_down = contract(hidden, group_cots, 0, 0).astype(jnp.bfloat16)
    grad_gate = contract(group_rows, gate_grad, 0, 0).astype(jnp.bfloat16)
    grad_up = contract(group_rows, up_grad, 0, 0).astype(jnp.bfloat16)
    whole_term = contract(gate_grad, gate_weight, 1, 1) + contract(up_grad, up_weight, 1, 1)
    row_grads = lax.psum_scatter(whole_term, "dp", scatter_dimension=0, tiled=True)
    row_grads = row_grads.astype(jnp.bfloat16)
    slot_grads = contract(chooser, row_grads, 0, 0).astype(jnp.bfloat16)
    slot_grads = slot_grads.reshape(expert_count, capacity, model_width)
    returned = lax.all_to_all(slot_grads, "expert", split_axis=0, concat_axis=0, tiled=True)
    grad_rows = returned.reshape(1, 1, expert_count, capacity, model_width)
    return (grad_rows, grad_gate[None], grad_up[None], grad_down[None])


def exchange_kernel(
    x_ref, cot_ref, counts_hbm, kept_ref, rank_ref, wg_ref, wu_ref, wd_ref,
    final_out, gate_out, up_out, down_out,
    slots, counts_ref,
    stage, pieces, order, split, spread, rows, w_in, w_down, acc_gu, acc_dh, sib_out, sib_in, part, regroup, unit, unit_in,
    z_send, z_recv, y_send, y_recv, sb_send, sb_recv,
    r1_send, r1_recv, r2_send, r2_recv, load_sem, slot_sem,
):
    s = lax.axis_index("expert")
    d = lax.axis_index("dp")
    z, y, c = d // 4, (d // 2) % 2, d % 2
    width = rows.shape[1]
    half = width // 2
    quarter = half // 4
    pair = half // 2

    def device(e, zz, yy, cc):
        return (e, zz * 4 + yy * 2 + cc)

    def remote(src, dst, send, recv, where):
        return pltpu.make_async_remote_copy(
            src_ref=src, dst_ref=dst, send_sem=send, recv_sem=recv, device_id=where,
            device_id_type=pl.DeviceIdType.MESH,
        )

    others = [(de, dz, dy) for dz in (2, 3, 1, 0) for de in (1, 0) for dy in (1, 0) if (de, dz, dy) != (0, 0, 0)]

    def other_device(de, dz, dy):
        return device((s + de) % 2, (z + dz) % 4, (y + dy) % 2, c)

    slot_loads = [
        pltpu.make_async_copy(x_ref.at[0, 0], slots.at[0], slot_sem.at[0]),
        pltpu.make_async_copy(cot_ref.at[0, 0], slots.at[1], slot_sem.at[1]),
        pltpu.make_async_copy(counts_hbm, counts_ref, slot_sem.at[2]),
    ]
    loads = [
        pltpu.make_async_copy(wg_ref.at[0], w_in.at[:, pl.ds(0, 128)], load_sem.at[0]),
        pltpu.make_async_copy(wu_ref.at[0], w_in.at[:, pl.ds(128, 128)], load_sem.at[1]),
        pltpu.make_async_copy(wd_ref.at[0], w_down, load_sem.at[2]),
    ]
    barrier = pltpu.get_barrier_semaphore()
    greeted = [device(s, z, y, 1 - c)] + [other_device(*other) for other in others]
    for where in greeted:
        pl.semaphore_signal(barrier, inc=1, device_id=where, device_id_type=pl.DeviceIdType.MESH)
    for load in slot_loads + loads:
        load.start()
    for load in slot_loads:
        load.wait()

    row8 = lax.broadcasted_iota(jnp.int32, (8, quarter), 0)
    for e in range(2):
        live = jnp.where(s == 0, counts_ref[0, 0, e], counts_ref[1, 0, e])
        for t in range(2):
            source = slots[t, e].astype(jnp.float32)
            groups = []
            for k in range(2):
                value = jnp.zeros((8, quarter), jnp.float32)
                for g in range(8):
                    line = source[k:k + 1, g * quarter:(g + 1) * quarter]
                    value = jnp.where(row8 == g, jnp.broadcast_to(line, value.shape), value)
                groups.append(value * jnp.where(k < live, 1.0, 0.0).astype(jnp.float32))
            stage[e, t * 16:(t + 1) * 16, :] = jnp.concatenate(groups, axis=0).astype(jnp.bfloat16)

    pl.semaphore_wait(barrier, len(greeted))

    sends = []

    def piece(ss, zz, yy, cc):
        return pieces.at[yy * 2 + cc, pl.ds(pl.multiple_of((zz * 2 + ss) * 32, 32), 32), :]

    def forward(ref, send, recv, where):
        copy = remote(ref, ref, send, recv, where)
        copy.start()
        sends.append(copy)
        return copy

    sibling = device(s, z, y, 1 - c)
    opposite = device(s, z, 1 - y, c)
    own_rows = pl.ds(pl.multiple_of((z * 2 + s) * 32, 32), 32)
    pieces[y * 2 + c, own_rows, :] = stage[s]
    own = piece(s, z, y, c)
    y_copies = [forward(own, y_send.at[0], y_recv.at[0], opposite)]
    line = [(1, 0), (0, 1), (1, 1), (0, 3), (1, 3), (0, 2), (1, 2)]
    z_copies = {}
    for de, dz in line[:1] + line[:0:-1]:
        index = de * 4 + dz
        copy = remote(
            stage.at[(s + de) % 2], piece(s, z, y, c), z_send.at[index], z_recv.at[index], other_device(de, dz, 0)
        )
        copy.start()
        z_copies[de, dz] = copy
        sends.append(copy)
    s_copies = [forward(own, sb_send.at[0], sb_recv.at[0], sibling)]

    i = lax.broadcasted_iota(jnp.int32, (256, 256), 0)
    j = lax.broadcasted_iota(jnp.int32, (256, 256), 1)
    order[...] = (
        ((i >> 5) == (j & 7))
        & (((i >> 4) & 1) == ((j >> 4) & 1))
        & (((i >> 2) & 3) == (j >> 6))
        & (((i >> 1) & 1) == ((j >> 5) & 1))
        & ((i & 1) == ((j >> 3) & 1))
    ).astype(jnp.float32).astype(jnp.bfloat16)
    si = lax.broadcasted_iota(jnp.int32, (64, 64), 0)
    sj = lax.broadcasted_iota(jnp.int32, (64, 64), 1)
    split[...] = (
        ((sj >> 5) == ((si & 31) >> 4))
        & ((sj & 15) == (si & 15))
        & (((sj >> 4) & 1) == jnp.where(si >= 32, c, 1 - c))
    ).astype(jnp.float32).astype(jnp.bfloat16)
    spread[...] = (
        ((j >> 5) == ((i >> 1) & 7))
        & ((j & 1) == (i & 1))
        & (((j >> 1) & 1) == ((i >> 4) & 1))
        & (((j >> 2) & 7) == (i >> 5))
    ).astype(jnp.float32).astype(jnp.bfloat16)

    for de, dz in line:
        z_copies[de, dz].wait_recv()
        index = de * 4 + dz
        got = piece((s + de) % 2, (z + 4 - dz) % 4, y, c)
        y_copies.append(forward(got, y_send.at[index], y_recv.at[index], opposite))
        s_copies.append(forward(got, sb_send.at[index], sb_recv.at[index], sibling))

    for load in loads:
        load.wait()

    def arrange(yy, cc):
        ordered = jnp.dot(order[...], pieces[yy * 2 + cc], preferred_element_type=jnp.float32).astype(jnp.bfloat16)
        place = pl.ds(pl.multiple_of((yy * 2 + cc) * 32, 32), 32)
        for g in range(8):
            rows[place, g * quarter:(g + 1) * quarter] = ordered[g * 32:(g + 1) * 32, :]

    def forward_part(yy, start, stop):
        some = rows[pl.ds(pl.multiple_of(yy * 64, 64), 64), start:stop]
        both = jnp.dot(some, w_in[start:stop, :], preferred_element_type=jnp.float32)
        back = lax.dot_general(
            some, w_down[:, start:stop], (((1,), (1,)), ((), ())), preferred_element_type=jnp.float32
        )
        both = both.reshape(2, 32, 256)[:, 0:16].reshape(32, 256)
        back = back.reshape(2, 32, 128)[:, 16:32].reshape(32, 128)
        place = pl.ds(pl.multiple_of(yy * 32, 32), 32)
        if start > 0:
            both = both + acc_gu[place, :]
            back = back + acc_dh[place, :]
        acc_gu[place, :] = both
        acc_dh[place, :] = back

    last = []

    def pass_on(n):
        y_copies[n].wait_recv()
        de, dz = ([(0, 0)] + line)[n]
        got = piece((s + de) % 2, (z + 4 - dz) % 4, 1 - y, c)
        index = 8 + de * 4 + dz
        last.append(forward(got, sb_send.at[index], sb_recv.at[index], sibling))

    arrange(y, c)
    for n in range(4):
        pass_on(n)
    for copy in s_copies:
        copy.wait_recv()
    arrange(y, 1 - c)
    forward_part(y, 0, half)
    for n in range(4, 8):
        pass_on(n)
    arrange(1 - y, c)
    forward_part(y, half, width)
    for copy in last:
        copy.wait_recv()
    arrange(1 - y, 1 - c)
    forward_part(1 - y, 0, width)

    keep = jnp.where(rank_ref[0, 0] < kept_ref[0], 1.0, 0.0).astype(jnp.float32)
    gate_pre = acc_gu[:, 0:128]
    up_pre = acc_gu[:, 128:256]
    hidden_grad = acc_dh[...]
    sigmoid_gate = jax.nn.sigmoid(gate_pre)
    activated = gate_pre * sigmoid_gate
    hidden = activated * up_pre * keep
    up_grad = hidden_grad * activated * keep
    gate_grad = hidden_grad * up_pre * sigmoid_gate * (1.0 + gate_pre * (1.0 - sigmoid_gate)) * keep
    both_grad = jnp.concatenate([gate_grad, up_grad], axis=1)
    both_bf16 = both_grad.astype(jnp.bfloat16)

    by_core = jnp.dot(split[...], both_bf16, preferred_element_type=jnp.float32).astype(jnp.bfloat16)
    sib_copies = []
    for n in range(4):
        term = lax.dot_general(
            by_core, w_in[n * pair:(n + 1) * pair, :], (((1,), (1,)), ((), ())), preferred_element_type=jnp.float32
        )
        sib_out[n] = term[0:32].astype(jnp.bfloat16)
        copy = remote(sib_out.at[n], sib_in.at[n], r1_send.at[n], r1_recv.at[n], sibling)
        copy.start()
        sib_copies.append(copy)
        part[n] = term[32:64]
    sends += sib_copies

    zeros = jnp.zeros((4, 16, 128), jnp.float32)
    hidden_pad = jnp.concatenate([zeros, hidden.reshape(4, 16, 128)], axis=1).reshape(128, 128).astype(jnp.bfloat16)
    zeros2 = jnp.zeros((4, 16, 256), jnp.float32)
    both_pad = jnp.concatenate([both_grad.reshape(4, 16, 256), zeros2], axis=1).reshape(128, 256).astype(jnp.bfloat16)

    for n in range(4):
        columns = pl.ds(n * pair, pair)
        down_out[0, :, columns] = lax.dot_general(
            hidden_pad, rows[:, columns], (((0,), (0,)), ((), ())), preferred_element_type=jnp.float32
        ).astype(jnp.bfloat16)

    for n in range(4):
        sib_copies[n].wait_recv()
        total = (part[n] + sib_in[n].astype(jnp.float32)).astype(jnp.bfloat16)
        regroup[n * 64:n * 64 + 32, :] = total[:, 0:quarter]
        regroup[n * 64 + 32:n * 64 + 64, :] = total[:, quarter:]
    unit[...] = jnp.dot(spread[...], regroup[...], preferred_element_type=jnp.float32).astype(jnp.bfloat16)

    def unit_of(ee, zz, yy):
        return unit.at[pl.ds(pl.multiple_of(((yy * 4 + zz) * 2 + ee) * 16, 16), 16), :]

    unit_copies = []
    for de, dz, dy in others:
        index = de * 8 + dz * 2 + dy
        copy = remote(
            unit_of((s + de) % 2, (z + dz) % 4, (y + dy) % 2), unit_in.at[index],
            r2_send.at[index], r2_recv.at[index], other_device(de, dz, dy),
        )
        copy.start()
        unit_copies.append(copy)
    sends += unit_copies

    for n in range(4):
        columns = pl.ds(n * pair, pair)
        some = rows[:, columns]
        inner = lax.dot_general(
            some, both_pad, (((0,), (0,)), ((), ())), preferred_element_type=jnp.float32
        ).astype(jnp.bfloat16)
        gate_out[0, columns, :] = inner[:, 0:128]
        up_out[0, columns, :] = inner[:, 128:256]

    for copy in unit_copies:
        copy.wait_recv()
    for de in range(2):
        if de == 0:
            result = unit[pl.ds(pl.multiple_of(((y * 4 + z) * 2 + s) * 16, 16), 16), :].astype(jnp.float32)
        else:
            result = unit_in[8].astype(jnp.float32)
        for index in range(1, 8):
            result = result + unit_in[de * 8 + index].astype(jnp.float32)
        final_out[pl.ds(pl.multiple_of(((s + de) % 2) * 16, 16), 16), :] = result.astype(jnp.bfloat16)
    for copy in sends:
        copy.wait_send()


def finish_kernel(final_ref, gate_ref, up_ref, down_ref, rows_out, gate_out, up_out, down_out, lines, sem, line_sem):
    copies = []
    depth = gate_ref.shape[1] // 4
    lanes = down_ref.shape[1] // 4
    for n in range(4):
        some = pl.ds(n * depth, depth)
        few = pl.ds(n * lanes, lanes)
        copies += [
            pltpu.make_async_copy(gate_ref.at[:, some, :], gate_out.at[:, some, :], sem.at[n]),
            pltpu.make_async_copy(up_ref.at[:, some, :], up_out.at[:, some, :], sem.at[4 + n]),
            pltpu.make_async_copy(down_ref.at[:, few, :], down_out.at[:, few, :], sem.at[8 + n]),
        ]
    for copy in copies:
        copy.start()
    quarter = final_ref.shape[1]
    final = final_ref[...].astype(jnp.float32)
    for e in range(2):
        for g in range(8):
            start = e * 16 + g * 2
            lines[0, 0, e, :, g * quarter:(g + 1) * quarter] = final[start:start + 2, :].astype(jnp.bfloat16)
    line_copy = pltpu.make_async_copy(lines, rows_out, line_sem)
    line_copy.start()
    for copy in copies:
        copy.wait()
    line_copy.wait()


def kernel_body(x_rows, cot_rows, counts, w_gate, w_up, w_down, kept_blocks, block_rank):
    width = x_rows.shape[4]
    quarter = width // 8
    pair = width // 4

    vmem = pl.BlockSpec(memory_space=pltpu.VMEM)
    hbm = pl.BlockSpec(memory_space=pltpu.HBM)
    anywhere = pl.BlockSpec(memory_space=pl.ANY)
    smem = pl.BlockSpec(memory_space=pltpu.SMEM)
    held = [
        pltpu.with_memory_space_constraint(a, pltpu.HBM) for a in (x_rows, cot_rows, counts, w_gate, w_up, w_down)
    ]
    bf16, f32 = jnp.bfloat16, jnp.float32
    dma = pltpu.SemaphoreType.DMA
    final_rows, grad_gate, grad_up, grad_down = pl.pallas_call(
        exchange_kernel,
        out_shape=(
            jax.ShapeDtypeStruct((32, quarter), bf16),
            jax.ShapeDtypeStruct(w_gate.shape, bf16),
            jax.ShapeDtypeStruct(w_up.shape, bf16),
            jax.ShapeDtypeStruct(w_down.shape, bf16),
        ),
        in_specs=[hbm, hbm, hbm, smem, smem, hbm, hbm, hbm],
        out_specs=(vmem, vmem, vmem, vmem),
        scratch_shapes=[
            pltpu.VMEM((2,) + x_rows.shape[2:], bf16),
            pltpu.SMEM(counts.shape, jnp.int32),
            pltpu.VMEM((2, 32, quarter), bf16),
            pltpu.VMEM((4, 256, quarter), bf16),
            pltpu.VMEM((256, 256), bf16),
            pltpu.VMEM((64, 64), bf16),
            pltpu.VMEM((256, 256), bf16),
            pltpu.VMEM((128, width), bf16),
            pltpu.VMEM((width, 256), bf16),
            pltpu.VMEM((128, width), bf16),
            pltpu.VMEM((64, 256), f32),
            pltpu.VMEM((64, 128), f32),
            pltpu.VMEM((4, 32, pair), bf16),
            pltpu.VMEM((4, 32, pair), bf16),
            pltpu.VMEM((4, 32, pair), f32),
            pltpu.VMEM((256, quarter), bf16),
            pltpu.VMEM((256, quarter), bf16),
            pltpu.VMEM((16, 16, quarter), bf16),
            dma((8,)), dma((8,)), dma((8,)), dma((8,)), dma((16,)), dma((16,)),
            dma((4,)), dma((4,)), dma((16,)), dma((16,)), dma((3,)), dma((3,)),
        ],
        compiler_params=pltpu.CompilerParams(
            collective_id=0, has_side_effects=True, vmem_limit_bytes=32 * 1024 * 1024
        ),
        name="expert_backward",
    )(*held[:3], kept_blocks, block_rank, *held[3:])
    return pl.pallas_call(
        finish_kernel,
        out_shape=tuple(jax.ShapeDtypeStruct(a.shape, bf16) for a in (x_rows, w_gate, w_up, w_down)),
        in_specs=[vmem, anywhere, anywhere, anywhere],
        out_specs=(anywhere, anywhere, anywhere, anywhere),
        scratch_shapes=[pltpu.VMEM(x_rows.shape, bf16), dma((12,)), dma(())],
        compiler_params=pltpu.CompilerParams(vmem_limit_bytes=16 * 1024 * 1024),
        name="write_outputs",
    )(final_rows, grad_gate, grad_up, grad_down)


def solution(mesh):
    in_specs = (
        P("expert", "dp", None, None, None),
        P("expert", "dp", None, None, None),
        P(None, "dp", None),
        P("expert", None, "dp"),
        P("expert", None, "dp"),
        P("expert", "dp", None),
        P("expert"),
        P("expert", "dp"),
    )
    out_specs = (
        P("expert", "dp", None, None, None),
        P("expert", None, "dp"),
        P("expert", None, "dp"),
        P("expert", "dp", None),
    )
    small = mesh.shape["expert"] == 2 and mesh.shape["dp"] == 16
    return jax.shard_map(kernel_body if small else body, mesh=mesh, in_specs=in_specs, out_specs=out_specs, check_vma=False)
```

```python
import jax
import jax.numpy as jnp
from jax import lax
from jax.experimental import pallas as pl
from jax.experimental.pallas import tpu as pltpu
from jax.sharding import PartitionSpec as P

LIVE = 4


def compact_matrix(slot_counts, live_rows, capacity):
    sources = slot_counts.shape[0]
    within_slot = jnp.tile(jnp.arange(capacity, dtype=jnp.int32), sources)
    count_slot = jnp.repeat(slot_counts, capacity)
    offsets = jnp.repeat(jnp.cumsum(slot_counts) - slot_counts, capacity)
    target = offsets + within_slot
    alive = within_slot < count_slot
    row_index = jnp.arange(live_rows, dtype=jnp.int32)[:, None]
    return ((row_index == target[None, :]) & alive[None, :]).astype(jnp.bfloat16)


def contract(left, right, left_dim, right_dim):
    return lax.dot_general(
        left, right, (((left_dim,), (right_dim,)), ((), ())), preferred_element_type=jnp.float32
    )


def body(x_rows, cot_rows, counts, w_gate, w_up, w_down, kept_blocks, block_rank):
    expert_count = x_rows.shape[2]
    capacity = x_rows.shape[3]
    model_width = x_rows.shape[4]
    slot_rows = x_rows.reshape(expert_count, capacity, model_width)
    slot_cots = cot_rows.reshape(expert_count, capacity, model_width)
    my_expert = lax.axis_index("expert")
    picked = jnp.arange(expert_count, dtype=jnp.int32)[None, :] == my_expert
    own_counts = jnp.sum(jnp.where(picked, counts[:, 0, :], 0), axis=1)
    chooser = compact_matrix(own_counts, LIVE, capacity)

    def pack_rows(received):
        flat_rows = received.reshape(-1, model_width)
        return jnp.dot(chooser, flat_rows, preferred_element_type=jnp.float32).astype(jnp.bfloat16)

    got_rows, got_cots = (
        lax.all_to_all(slot_rows, "expert", split_axis=0, concat_axis=0, tiled=True),
        lax.all_to_all(slot_cots, "expert", split_axis=0, concat_axis=0, tiled=True),
    )
    group_rows, group_cots = (
        lax.all_gather(pack_rows(got_rows), "dp", axis=0, tiled=True),
        lax.all_gather(pack_rows(got_cots), "dp", axis=0, tiled=True),
    )
    gate_weight = w_gate[0]
    up_weight = w_up[0]
    down_weight = w_down[0]
    keep_mask = (block_rank.reshape(()) < kept_blocks.reshape(())).astype(jnp.float32)
    gate_pre = jnp.dot(group_rows, gate_weight, preferred_element_type=jnp.float32)
    up_pre = jnp.dot(group_rows, up_weight, preferred_element_type=jnp.float32)
    sigmoid_gate = jax.nn.sigmoid(gate_pre)
    activated = gate_pre * sigmoid_gate
    hidden = (activated * up_pre * keep_mask).astype(jnp.bfloat16)
    hidden_grad = contract(group_cots, down_weight, 1, 1)
    up_grad = (hidden_grad * activated * keep_mask).astype(jnp.bfloat16)
    gate_grad = (
        hidden_grad * up_pre * sigmoid_gate * (1.0 + gate_pre * (1.0 - sigmoid_gate)) * keep_mask
    ).astype(jnp.bfloat16)
    grad_down = contract(hidden, group_cots, 0, 0).astype(jnp.bfloat16)
    grad_gate = contract(group_rows, gate_grad, 0, 0).astype(jnp.bfloat16)
    grad_up = contract(group_rows, up_grad, 0, 0).astype(jnp.bfloat16)
    whole_term = contract(gate_grad, gate_weight, 1, 1) + contract(up_grad, up_weight, 1, 1)
    row_grads = lax.psum_scatter(whole_term, "dp", scatter_dimension=0, tiled=True)
    row_grads = row_grads.astype(jnp.bfloat16)
    slot_grads = contract(chooser, row_grads, 0, 0).astype(jnp.bfloat16)
    slot_grads = slot_grads.reshape(expert_count, capacity, model_width)
    returned = lax.all_to_all(slot_grads, "expert", split_axis=0, concat_axis=0, tiled=True)
    grad_rows = returned.reshape(1, 1, expert_count, capacity, model_width)
    return (grad_rows, grad_gate[None], grad_up[None], grad_down[None])


def exchange_kernel(
    x_ref, cot_ref, counts_hbm, kept_ref, rank_ref, wg_ref, wu_ref, wd_ref,
    final_out, gate_out, up_out, down_out,
    slots, counts_ref,
    stage, pieces, order, split, spread, rows, w_in, w_turned, w_down, acc_gu, acc_dh, sib_out, sib_in, part, regroup, unit, unit_in,
    z_send, z_recv, y_send, y_recv, sb_send, sb_recv,
    r1_send, r1_recv, r2_send, r2_recv, load_sem, slot_sem,
):
    s = lax.axis_index("expert")
    d = lax.axis_index("dp")
    z, y, c = d // 4, (d // 2) % 2, d % 2
    width = rows.shape[1]
    half = width // 2
    quarter = half // 4
    pair = half // 2

    def device(e, zz, yy, cc):
        return (e, zz * 4 + yy * 2 + cc)

    def remote(src, dst, send, recv, where):
        return pltpu.make_async_remote_copy(
            src_ref=src, dst_ref=dst, send_sem=send, recv_sem=recv, device_id=where,
            device_id_type=pl.DeviceIdType.MESH,
        )

    others = [(de, dz, dy) for dz in (2, 3, 1, 0) for de in (1, 0) for dy in (1, 0) if (de, dz, dy) != (0, 0, 0)]

    def other_device(de, dz, dy):
        return device((s + de) % 2, (z + dz) % 4, (y + dy) % 2, c)

    slot_loads = [
        pltpu.make_async_copy(x_ref.at[0, 0], slots.at[0], slot_sem.at[0]),
        pltpu.make_async_copy(cot_ref.at[0, 0], slots.at[1], slot_sem.at[1]),
        pltpu.make_async_copy(counts_hbm, counts_ref, slot_sem.at[2]),
    ]
    loads = [
        pltpu.make_async_copy(wg_ref.at[0], w_in.at[:, pl.ds(0, 128)], load_sem.at[0]),
        pltpu.make_async_copy(wu_ref.at[0], w_in.at[:, pl.ds(128, 128)], load_sem.at[1]),
        pltpu.make_async_copy(wd_ref.at[0], w_down, load_sem.at[2]),
    ]
    barrier = pltpu.get_barrier_semaphore()
    greeted = [device(s, z, y, 1 - c)] + [other_device(*other) for other in others]
    for where in greeted:
        pl.semaphore_signal(barrier, inc=1, device_id=where, device_id_type=pl.DeviceIdType.MESH)
    for load in slot_loads + loads:
        load.start()
    for load in slot_loads:
        load.wait()

    row8 = lax.broadcasted_iota(jnp.int32, (8, quarter), 0)
    for e in range(2):
        live = jnp.where(s == 0, counts_ref[0, 0, e], counts_ref[1, 0, e])
        for t in range(2):
            source = slots[t, e].astype(jnp.float32)
            groups = []
            for k in range(2):
                value = jnp.zeros((8, quarter), jnp.float32)
                for g in range(8):
                    line = source[k:k + 1, g * quarter:(g + 1) * quarter]
                    value = jnp.where(row8 == g, jnp.broadcast_to(line, value.shape), value)
                groups.append(value * jnp.where(k < live, 1.0, 0.0).astype(jnp.float32))
            stage[e, t * 16:(t + 1) * 16, :] = jnp.concatenate(groups, axis=0).astype(jnp.bfloat16)

    pl.semaphore_wait(barrier, len(greeted))

    sends = []

    def piece(ss, zz, yy, cc):
        return pieces.at[yy * 2 + cc, pl.ds(pl.multiple_of((zz * 2 + ss) * 32, 32), 32), :]

    def forward(ref, send, recv, where):
        copy = remote(ref, ref, send, recv, where)
        copy.start()
        sends.append(copy)
        return copy

    sibling = device(s, z, y, 1 - c)
    opposite = device(s, z, 1 - y, c)
    own_rows = pl.ds(pl.multiple_of((z * 2 + s) * 32, 32), 32)
    pieces[y * 2 + c, own_rows, :] = stage[s]
    own = piece(s, z, y, c)
    y_copies = [forward(own, y_send.at[0], y_recv.at[0], opposite)]
    line = [(1, 0), (0, 1), (1, 1), (0, 3), (1, 3), (0, 2), (1, 2)]
    z_copies = {}
    for de, dz in line[:1] + line[:0:-1]:
        index = de * 4 + dz
        copy = remote(
            stage.at[(s + de) % 2], piece(s, z, y, c), z_send.at[index], z_recv.at[index], other_device(de, dz, 0)
        )
        copy.start()
        z_copies[de, dz] = copy
        sends.append(copy)
    s_copies = [forward(own, sb_send.at[0], sb_recv.at[0], sibling)]

    i = lax.broadcasted_iota(jnp.int32, (256, 256), 0)
    j = lax.broadcasted_iota(jnp.int32, (256, 256), 1)
    order[...] = (
        ((i >> 5) == (j & 7))
        & (((i >> 4) & 1) == ((j >> 4) & 1))
        & (((i >> 2) & 3) == (j >> 6))
        & (((i >> 1) & 1) == ((j >> 5) & 1))
        & ((i & 1) == ((j >> 3) & 1))
    ).astype(jnp.float32).astype(jnp.bfloat16)
    si = lax.broadcasted_iota(jnp.int32, (64, 64), 0)
    sj = lax.broadcasted_iota(jnp.int32, (64, 64), 1)
    split[...] = (
        ((sj >> 5) == ((si & 31) >> 4))
        & ((sj & 15) == (si & 15))
        & (((sj >> 4) & 1) == jnp.where(si >= 32, c, 1 - c))
    ).astype(jnp.float32).astype(jnp.bfloat16)
    spread[...] = (
        ((j >> 5) == ((i >> 1) & 7))
        & ((j & 1) == (i & 1))
        & (((j >> 1) & 1) == ((i >> 4) & 1))
        & (((j >> 2) & 7) == (i >> 5))
    ).astype(jnp.float32).astype(jnp.bfloat16)

    for load in loads:
        load.wait()

    def turn(n):
        some = pl.ds(n * quarter, quarter)
        w_turned[:, some] = w_in[some, 0:256].T
        w_in[some, 256:384] = w_down[:, some].T

    turn(0)
    for n, (de, dz) in enumerate(line):
        z_copies[de, dz].wait_recv()
        index = de * 4 + dz
        got = piece((s + de) % 2, (z + 4 - dz) % 4, y, c)
        y_copies.append(forward(got, y_send.at[index], y_recv.at[index], opposite))
        s_copies.append(forward(got, sb_send.at[index], sb_recv.at[index], sibling))
        turn(n + 1)

    def arrange(yy, cc):
        ordered = jnp.dot(order[...], pieces[yy * 2 + cc], preferred_element_type=jnp.float32).astype(jnp.bfloat16)
        place = pl.ds(pl.multiple_of((yy * 2 + cc) * 32, 32), 32)
        for g in range(8):
            rows[place, g * quarter:(g + 1) * quarter] = ordered[g * 32:(g + 1) * 32, :]

    def forward_part(yy, start, stop):
        some = rows[pl.ds(pl.multiple_of(yy * 64, 64), 64), start:stop]
        out = jnp.dot(some, w_in[start:stop, :], preferred_element_type=jnp.float32)
        both = out[:, 0:256].reshape(2, 32, 256)[:, 0:16].reshape(32, 256)
        back = out[:, 256:384].reshape(2, 32, 128)[:, 16:32].reshape(32, 128)
        place = pl.ds(pl.multiple_of(yy * 32, 32), 32)
        if start > 0:
            both = both + acc_gu[place, :]
            back = back + acc_dh[place, :]
        acc_gu[place, :] = both
        acc_dh[place, :] = back

    last = []

    def pass_on(n):
        y_copies[n].wait_recv()
        de, dz = ([(0, 0)] + line)[n]
        got = piece((s + de) % 2, (z + 4 - dz) % 4, 1 - y, c)
        index = 8 + de * 4 + dz
        last.append(forward(got, sb_send.at[index], sb_recv.at[index], sibling))

    arrange(y, c)
    for n in range(4):
        pass_on(n)
    for copy in s_copies:
        copy.wait_recv()
    arrange(y, 1 - c)
    forward_part(y, 0, half)
    for n in range(4, 8):
        pass_on(n)
    arrange(1 - y, c)
    forward_part(y, half, width)
    for copy in last:
        copy.wait_recv()
    arrange(1 - y, 1 - c)
    forward_part(1 - y, 0, width)

    keep = jnp.where(rank_ref[0, 0] < kept_ref[0], 1.0, 0.0).astype(jnp.float32)
    gate_pre = acc_gu[:, 0:128]
    up_pre = acc_gu[:, 128:256]
    hidden_grad = acc_dh[...]
    sigmoid_gate = jax.nn.sigmoid(gate_pre)
    activated = gate_pre * sigmoid_gate
    hidden = activated * up_pre * keep
    up_grad = hidden_grad * activated * keep
    gate_grad = hidden_grad * up_pre * sigmoid_gate * (1.0 + gate_pre * (1.0 - sigmoid_gate)) * keep
    both_grad = jnp.concatenate([gate_grad, up_grad], axis=1)
    both_bf16 = both_grad.astype(jnp.bfloat16)

    by_core = jnp.dot(split[...], both_bf16, preferred_element_type=jnp.float32).astype(jnp.bfloat16)
    sib_copies = []
    for n in range(4):
        term = jnp.dot(by_core, w_turned[:, n * pair:(n + 1) * pair], preferred_element_type=jnp.float32)
        sib_out[n] = term[0:32].astype(jnp.bfloat16)
        copy = remote(sib_out.at[n], sib_in.at[n], r1_send.at[n], r1_recv.at[n], sibling)
        copy.start()
        sib_copies.append(copy)
        part[n] = term[32:64]
    sends += sib_copies

    zeros = jnp.zeros((4, 16, 128), jnp.float32)
    hidden_pad = jnp.concatenate([zeros, hidden.reshape(4, 16, 128)], axis=1).reshape(128, 128).astype(jnp.bfloat16)
    zeros2 = jnp.zeros((4, 16, 256), jnp.float32)
    both_pad = jnp.concatenate([both_grad.reshape(4, 16, 256), zeros2], axis=1).reshape(128, 256).astype(jnp.bfloat16)

    for n in range(4):
        sib_copies[n].wait_recv()
        total = (part[n] + sib_in[n].astype(jnp.float32)).astype(jnp.bfloat16)
        regroup[n * 64:n * 64 + 32, :] = total[:, 0:quarter]
        regroup[n * 64 + 32:n * 64 + 64, :] = total[:, quarter:]
    unit[...] = jnp.dot(spread[...], regroup[...], preferred_element_type=jnp.float32).astype(jnp.bfloat16)

    def unit_of(ee, zz, yy):
        return unit.at[pl.ds(pl.multiple_of(((yy * 4 + zz) * 2 + ee) * 16, 16), 16), :]

    unit_copies = []
    for de, dz, dy in others:
        index = de * 8 + dz * 2 + dy
        copy = remote(
            unit_of((s + de) % 2, (z + dz) % 4, (y + dy) % 2), unit_in.at[index],
            r2_send.at[index], r2_recv.at[index], other_device(de, dz, dy),
        )
        copy.start()
        unit_copies.append(copy)
    sends += unit_copies

    for n in range(4):
        columns = pl.ds(n * pair, pair)
        some = rows[:, columns]
        down_out[0, :, columns] = lax.dot_general(
            hidden_pad, some, (((0,), (0,)), ((), ())), preferred_element_type=jnp.float32
        ).astype(jnp.bfloat16)
        inner = lax.dot_general(
            some, both_pad, (((0,), (0,)), ((), ())), preferred_element_type=jnp.float32
        ).astype(jnp.bfloat16)
        gate_out[0, columns, :] = inner[:, 0:128]
        up_out[0, columns, :] = inner[:, 128:256]

    for copy in unit_copies:
        copy.wait_recv()
    for de in range(2):
        if de == 0:
            result = unit[pl.ds(pl.multiple_of(((y * 4 + z) * 2 + s) * 16, 16), 16), :].astype(jnp.float32)
        else:
            result = unit_in[8].astype(jnp.float32)
        for index in range(1, 8):
            result = result + unit_in[de * 8 + index].astype(jnp.float32)
        final_out[pl.ds(pl.multiple_of(((s + de) % 2) * 16, 16), 16), :] = result.astype(jnp.bfloat16)
    for copy in sends:
        copy.wait_send()


def finish_kernel(final_ref, gate_ref, up_ref, down_ref, rows_out, gate_out, up_out, down_out, lines, sem, line_sem):
    copies = []
    depth = gate_ref.shape[1] // 4
    lanes = down_ref.shape[1] // 4
    for n in range(4):
        some = pl.ds(n * depth, depth)
        few = pl.ds(n * lanes, lanes)
        copies += [
            pltpu.make_async_copy(gate_ref.at[:, some, :], gate_out.at[:, some, :], sem.at[n]),
            pltpu.make_async_copy(up_ref.at[:, some, :], up_out.at[:, some, :], sem.at[4 + n]),
            pltpu.make_async_copy(down_ref.at[:, few, :], down_out.at[:, few, :], sem.at[8 + n]),
        ]
    for copy in copies:
        copy.start()
    quarter = final_ref.shape[1]
    final = final_ref[...].astype(jnp.float32)
    for e in range(2):
        for g in range(8):
            start = e * 16 + g * 2
            lines[0, 0, e, :, g * quarter:(g + 1) * quarter] = final[start:start + 2, :].astype(jnp.bfloat16)
    line_copy = pltpu.make_async_copy(lines, rows_out, line_sem)
    line_copy.start()
    for copy in copies:
        copy.wait()
    line_copy.wait()


def kernel_body(x_rows, cot_rows, counts, w_gate, w_up, w_down, kept_blocks, block_rank):
    width = x_rows.shape[4]
    quarter = width // 8
    pair = width // 4

    vmem = pl.BlockSpec(memory_space=pltpu.VMEM)
    hbm = pl.BlockSpec(memory_space=pltpu.HBM)
    anywhere = pl.BlockSpec(memory_space=pl.ANY)
    smem = pl.BlockSpec(memory_space=pltpu.SMEM)
    held = [
        pltpu.with_memory_space_constraint(a, pltpu.HBM) for a in (x_rows, cot_rows, counts, w_gate, w_up, w_down)
    ]
    bf16, f32 = jnp.bfloat16, jnp.float32
    dma = pltpu.SemaphoreType.DMA
    final_rows, grad_gate, grad_up, grad_down = pl.pallas_call(
        exchange_kernel,
        out_shape=(
            jax.ShapeDtypeStruct((32, quarter), bf16),
            jax.ShapeDtypeStruct(w_gate.shape, bf16),
            jax.ShapeDtypeStruct(w_up.shape, bf16),
            jax.ShapeDtypeStruct(w_down.shape, bf16),
        ),
        in_specs=[hbm, hbm, hbm, smem, smem, hbm, hbm, hbm],
        out_specs=(vmem, vmem, vmem, vmem),
        scratch_shapes=[
            pltpu.VMEM((2,) + x_rows.shape[2:], bf16),
            pltpu.SMEM(counts.shape, jnp.int32),
            pltpu.VMEM((2, 32, quarter), bf16),
            pltpu.VMEM((4, 256, quarter), bf16),
            pltpu.VMEM((256, 256), bf16),
            pltpu.VMEM((64, 64), bf16),
            pltpu.VMEM((256, 256), bf16),
            pltpu.VMEM((128, width), bf16),
            pltpu.VMEM((width, 384), bf16),
            pltpu.VMEM((256, width), bf16),
            pltpu.VMEM((128, width), bf16),
            pltpu.VMEM((64, 256), f32),
            pltpu.VMEM((64, 128), f32),
            pltpu.VMEM((4, 32, pair), bf16),
            pltpu.VMEM((4, 32, pair), bf16),
            pltpu.VMEM((4, 32, pair), f32),
            pltpu.VMEM((256, quarter), bf16),
            pltpu.VMEM((256, quarter), bf16),
            pltpu.VMEM((16, 16, quarter), bf16),
            dma((8,)), dma((8,)), dma((8,)), dma((8,)), dma((16,)), dma((16,)),
            dma((4,)), dma((4,)), dma((16,)), dma((16,)), dma((3,)), dma((3,)),
        ],
        compiler_params=pltpu.CompilerParams(
            collective_id=0, has_side_effects=True, vmem_limit_bytes=32 * 1024 * 1024
        ),
        name="expert_backward",
    )(*held[:3], kept_blocks, block_rank, *held[3:])
    return pl.pallas_call(
        finish_kernel,
        out_shape=tuple(jax.ShapeDtypeStruct(a.shape, bf16) for a in (x_rows, w_gate, w_up, w_down)),
        in_specs=[vmem, anywhere, anywhere, anywhere],
        out_specs=(anywhere, anywhere, anywhere, anywhere),
        scratch_shapes=[pltpu.VMEM(x_rows.shape, bf16), dma((12,)), dma(())],
        compiler_params=pltpu.CompilerParams(vmem_limit_bytes=16 * 1024 * 1024),
        name="write_outputs",
    )(final_rows, grad_gate, grad_up, grad_down)


def solution(mesh):
    in_specs = (
        P("expert", "dp", None, None, None),
        P("expert", "dp", None, None, None),
        P(None, "dp", None),
        P("expert", None, "dp"),
        P("expert", None, "dp"),
        P("expert", "dp", None),
        P("expert"),
        P("expert", "dp"),
    )
    out_specs = (
        P("expert", "dp", None, None, None),
        P("expert", None, "dp"),
        P("expert", None, "dp"),
        P("expert", "dp", None),
    )
    small = mesh.shape["expert"] == 2 and mesh.shape["dp"] == 16
    return jax.shard_map(kernel_body if small else body, mesh=mesh, in_specs=in_specs, out_specs=out_specs, check_vma=False)
```

```python
import jax
import jax.numpy as jnp
from jax import lax
from jax.experimental import pallas as pl
from jax.experimental.pallas import tpu as pltpu
from jax.sharding import PartitionSpec as P

LIVE = 4


def compact_matrix(slot_counts, live_rows, capacity):
    sources = slot_counts.shape[0]
    within_slot = jnp.tile(jnp.arange(capacity, dtype=jnp.int32), sources)
    count_slot = jnp.repeat(slot_counts, capacity)
    offsets = jnp.repeat(jnp.cumsum(slot_counts) - slot_counts, capacity)
    target = offsets + within_slot
    alive = within_slot < count_slot
    row_index = jnp.arange(live_rows, dtype=jnp.int32)[:, None]
    return ((row_index == target[None, :]) & alive[None, :]).astype(jnp.bfloat16)


def contract(left, right, left_dim, right_dim):
    return lax.dot_general(
        left, right, (((left_dim,), (right_dim,)), ((), ())), preferred_element_type=jnp.float32
    )


def body(x_rows, cot_rows, counts, w_gate, w_up, w_down, kept_blocks, block_rank):
    expert_count = x_rows.shape[2]
    capacity = x_rows.shape[3]
    model_width = x_rows.shape[4]
    slot_rows = x_rows.reshape(expert_count, capacity, model_width)
    slot_cots = cot_rows.reshape(expert_count, capacity, model_width)
    my_expert = lax.axis_index("expert")
    picked = jnp.arange(expert_count, dtype=jnp.int32)[None, :] == my_expert
    own_counts = jnp.sum(jnp.where(picked, counts[:, 0, :], 0), axis=1)
    chooser = compact_matrix(own_counts, LIVE, capacity)

    def pack_rows(received):
        flat_rows = received.reshape(-1, model_width)
        return jnp.dot(chooser, flat_rows, preferred_element_type=jnp.float32).astype(jnp.bfloat16)

    got_rows, got_cots = (
        lax.all_to_all(slot_rows, "expert", split_axis=0, concat_axis=0, tiled=True),
        lax.all_to_all(slot_cots, "expert", split_axis=0, concat_axis=0, tiled=True),
    )
    group_rows, group_cots = (
        lax.all_gather(pack_rows(got_rows), "dp", axis=0, tiled=True),
        lax.all_gather(pack_rows(got_cots), "dp", axis=0, tiled=True),
    )
    gate_weight = w_gate[0]
    up_weight = w_up[0]
    down_weight = w_down[0]
    keep_mask = (block_rank.reshape(()) < kept_blocks.reshape(())).astype(jnp.float32)
    gate_pre = jnp.dot(group_rows, gate_weight, preferred_element_type=jnp.float32)
    up_pre = jnp.dot(group_rows, up_weight, preferred_element_type=jnp.float32)
    sigmoid_gate = jax.nn.sigmoid(gate_pre)
    activated = gate_pre * sigmoid_gate
    hidden = (activated * up_pre * keep_mask).astype(jnp.bfloat16)
    hidden_grad = contract(group_cots, down_weight, 1, 1)
    up_grad = (hidden_grad * activated * keep_mask).astype(jnp.bfloat16)
    gate_grad = (
        hidden_grad * up_pre * sigmoid_gate * (1.0 + gate_pre * (1.0 - sigmoid_gate)) * keep_mask
    ).astype(jnp.bfloat16)
    grad_down = contract(hidden, group_cots, 0, 0).astype(jnp.bfloat16)
    grad_gate = contract(group_rows, gate_grad, 0, 0).astype(jnp.bfloat16)
    grad_up = contract(group_rows, up_grad, 0, 0).astype(jnp.bfloat16)
    whole_term = contract(gate_grad, gate_weight, 1, 1) + contract(up_grad, up_weight, 1, 1)
    row_grads = lax.psum_scatter(whole_term, "dp", scatter_dimension=0, tiled=True)
    row_grads = row_grads.astype(jnp.bfloat16)
    slot_grads = contract(chooser, row_grads, 0, 0).astype(jnp.bfloat16)
    slot_grads = slot_grads.reshape(expert_count, capacity, model_width)
    returned = lax.all_to_all(slot_grads, "expert", split_axis=0, concat_axis=0, tiled=True)
    grad_rows = returned.reshape(1, 1, expert_count, capacity, model_width)
    return (grad_rows, grad_gate[None], grad_up[None], grad_down[None])


def exchange_kernel(
    x_ref, cot_ref, counts_hbm, kept_ref, rank_ref, wg_ref, wu_ref, wd_ref,
    final_out, gate_out, up_out, down_out,
    slots, counts_ref,
    stage, pieces, order, split, spread, rows, w_in, w_turned, w_down, acc_gu, acc_dh, sib_out, sib_in, part, regroup, unit, unit_in,
    z_send, z_recv, y_send, y_recv, sb_send, sb_recv,
    r1_send, r1_recv, r2_send, r2_recv, load_sem, slot_sem,
):
    s = lax.axis_index("expert")
    d = lax.axis_index("dp")
    z, y, c = d // 4, (d // 2) % 2, d % 2
    width = rows.shape[1]
    half = width // 2
    quarter = half // 4
    pair = half // 2

    def device(e, zz, yy, cc):
        return (e, zz * 4 + yy * 2 + cc)

    def remote(src, dst, send, recv, where):
        return pltpu.make_async_remote_copy(
            src_ref=src, dst_ref=dst, send_sem=send, recv_sem=recv, device_id=where,
            device_id_type=pl.DeviceIdType.MESH,
        )

    others = [(de, dz, dy) for dz in (2, 3, 1, 0) for de in (1, 0) for dy in (1, 0) if (de, dz, dy) != (0, 0, 0)]

    def partner(dz):
        return [z, z + 1 - 2 * (z % 2), (z + 2) % 4, 3 - z][dz]

    def other_device(de, dz, dy):
        return device((s + de) % 2, partner(dz), (y + dy) % 2, c)

    slot_loads = [
        pltpu.make_async_copy(x_ref.at[0, 0], slots.at[0], slot_sem.at[0]),
        pltpu.make_async_copy(cot_ref.at[0, 0], slots.at[1], slot_sem.at[1]),
        pltpu.make_async_copy(counts_hbm, counts_ref, slot_sem.at[2]),
    ]
    loads = [
        pltpu.make_async_copy(wg_ref.at[0], w_in.at[:, pl.ds(0, 128)], load_sem.at[0]),
        pltpu.make_async_copy(wu_ref.at[0], w_in.at[:, pl.ds(128, 128)], load_sem.at[1]),
        pltpu.make_async_copy(wd_ref.at[0], w_down, load_sem.at[2]),
    ]
    barrier = pltpu.get_barrier_semaphore()
    greeted = [device(s, z, y, 1 - c)] + [other_device(*other) for other in others]
    for where in greeted:
        pl.semaphore_signal(barrier, inc=1, device_id=where, device_id_type=pl.DeviceIdType.MESH)
    for load in slot_loads + loads:
        load.start()
    for load in slot_loads:
        load.wait()

    row8 = lax.broadcasted_iota(jnp.int32, (8, quarter), 0)
    for e in range(2):
        live = jnp.where(s == 0, counts_ref[0, 0, e], counts_ref[1, 0, e])
        for t in range(2):
            source = slots[t, e].astype(jnp.float32)
            groups = []
            for k in range(2):
                value = jnp.zeros((8, quarter), jnp.float32)
                for g in range(8):
                    line = source[k:k + 1, g * quarter:(g + 1) * quarter]
                    value = jnp.where(row8 == g, jnp.broadcast_to(line, value.shape), value)
                groups.append(value * jnp.where(k < live, 1.0, 0.0).astype(jnp.float32))
            stage[e, t * 16:(t + 1) * 16, :] = jnp.concatenate(groups, axis=0).astype(jnp.bfloat16)

    pl.semaphore_wait(barrier, len(greeted))

    sends = []

    def piece(ss, zz, yy, cc):
        return pieces.at[yy * 2 + cc, pl.ds(pl.multiple_of((zz * 2 + ss) * 32, 32), 32), :]

    def forward(ref, send, recv, where):
        copy = remote(ref, ref, send, recv, where)
        copy.start()
        sends.append(copy)
        return copy

    sibling = device(s, z, y, 1 - c)
    opposite = device(s, z, 1 - y, c)
    own_rows = pl.ds(pl.multiple_of((z * 2 + s) * 32, 32), 32)
    pieces[y * 2 + c, own_rows, :] = stage[s]
    own = piece(s, z, y, c)
    y_copies = [forward(own, y_send.at[0], y_recv.at[0], opposite)]
    line = [(1, 0), (0, 1), (1, 1), (0, 3), (1, 3), (0, 2), (1, 2)]
    z_copies = {}
    for de, dz in line:
        index = de * 4 + dz
        copy = remote(
            stage.at[(s + de) % 2], piece(s, z, y, c), z_send.at[index], z_recv.at[index], other_device(de, dz, 0)
        )
        copy.start()
        z_copies[de, dz] = copy
        sends.append(copy)
    s_copies = [forward(own, sb_send.at[0], sb_recv.at[0], sibling)]

    i = lax.broadcasted_iota(jnp.int32, (256, 256), 0)
    j = lax.broadcasted_iota(jnp.int32, (256, 256), 1)
    order[...] = (
        ((i >> 5) == (j & 7))
        & (((i >> 4) & 1) == ((j >> 4) & 1))
        & (((i >> 2) & 3) == (j >> 6))
        & (((i >> 1) & 1) == ((j >> 5) & 1))
        & ((i & 1) == ((j >> 3) & 1))
    ).astype(jnp.float32).astype(jnp.bfloat16)
    si = lax.broadcasted_iota(jnp.int32, (64, 64), 0)
    sj = lax.broadcasted_iota(jnp.int32, (64, 64), 1)
    split[...] = (
        ((sj >> 5) == ((si & 31) >> 4))
        & ((sj & 15) == (si & 15))
        & (((sj >> 4) & 1) == jnp.where(si >= 32, c, 1 - c))
    ).astype(jnp.float32).astype(jnp.bfloat16)
    spread[...] = (
        ((j >> 5) == ((i >> 1) & 7))
        & ((j & 1) == (i & 1))
        & (((j >> 1) & 1) == ((i >> 4) & 1))
        & (((j >> 2) & 7) == (i >> 5))
    ).astype(jnp.float32).astype(jnp.bfloat16)

    for load in loads:
        load.wait()

    def turn(n):
        some = pl.ds(n * quarter, quarter)
        w_turned[:, some] = w_in[some, 0:256].T
        w_in[some, 256:384] = w_down[:, some].T

    turn(0)
    for n, (de, dz) in enumerate(line):
        z_copies[de, dz].wait_recv()
        index = de * 4 + dz
        got = piece((s + de) % 2, partner(dz), y, c)
        y_copies.append(forward(got, y_send.at[index], y_recv.at[index], opposite))
        s_copies.append(forward(got, sb_send.at[index], sb_recv.at[index], sibling))
        turn(n + 1)

    def arrange(yy, cc):
        ordered = jnp.dot(order[...], pieces[yy * 2 + cc], preferred_element_type=jnp.float32).astype(jnp.bfloat16)
        place = pl.ds(pl.multiple_of((yy * 2 + cc) * 32, 32), 32)
        for g in range(8):
            rows[place, g * quarter:(g + 1) * quarter] = ordered[g * 32:(g + 1) * 32, :]

    def forward_part(yy, start, stop):
        some = rows[pl.ds(pl.multiple_of(yy * 64, 64), 64), start:stop]
        out = jnp.dot(some, w_in[start:stop, :], preferred_element_type=jnp.float32)
        both = out[:, 0:256].reshape(2, 32, 256)[:, 0:16].reshape(32, 256)
        back = out[:, 256:384].reshape(2, 32, 128)[:, 16:32].reshape(32, 128)
        place = pl.ds(pl.multiple_of(yy * 32, 32), 32)
        if start > 0:
            both = both + acc_gu[place, :]
            back = back + acc_dh[place, :]
        acc_gu[place, :] = both
        acc_dh[place, :] = back

    last = []

    def pass_on(n):
        y_copies[n].wait_recv()
        de, dz = ([(0, 0)] + line)[n]
        got = piece((s + de) % 2, partner(dz), 1 - y, c)
        index = 8 + de * 4 + dz
        last.append(forward(got, sb_send.at[index], sb_recv.at[index], sibling))

    arrange(y, c)
    for n in range(4):
        pass_on(n)
    for copy in s_copies:
        copy.wait_recv()
    arrange(y, 1 - c)
    forward_part(y, 0, half)
    for n in range(4, 8):
        pass_on(n)
    arrange(1 - y, c)
    forward_part(y, half, width)
    for copy in last:
        copy.wait_recv()
    arrange(1 - y, 1 - c)
    forward_part(1 - y, 0, width)

    keep = jnp.where(rank_ref[0, 0] < kept_ref[0], 1.0, 0.0).astype(jnp.float32)
    gate_pre = acc_gu[:, 0:128]
    up_pre = acc_gu[:, 128:256]
    hidden_grad = acc_dh[...]
    sigmoid_gate = jax.nn.sigmoid(gate_pre)
    activated = gate_pre * sigmoid_gate
    hidden = activated * up_pre * keep
    up_grad = hidden_grad * activated * keep
    gate_grad = hidden_grad * up_pre * sigmoid_gate * (1.0 + gate_pre * (1.0 - sigmoid_gate)) * keep
    both_grad = jnp.concatenate([gate_grad, up_grad], axis=1)
    both_bf16 = both_grad.astype(jnp.bfloat16)

    by_core = jnp.dot(split[...], both_bf16, preferred_element_type=jnp.float32).astype(jnp.bfloat16)
    sib_copies = []
    for n in range(4):
        term = jnp.dot(by_core, w_turned[:, n * pair:(n + 1) * pair], preferred_element_type=jnp.float32)
        sib_out[n] = term[0:32].astype(jnp.bfloat16)
        copy = remote(sib_out.at[n], sib_in.at[n], r1_send.at[n], r1_recv.at[n], sibling)
        copy.start()
        sib_copies.append(copy)
        part[n] = term[32:64]
    sends += sib_copies

    zeros = jnp.zeros((4, 16, 128), jnp.float32)
    hidden_pad = jnp.concatenate([zeros, hidden.reshape(4, 16, 128)], axis=1).reshape(128, 128).astype(jnp.bfloat16)
    zeros2 = jnp.zeros((4, 16, 256), jnp.float32)
    both_pad = jnp.concatenate([both_grad.reshape(4, 16, 256), zeros2], axis=1).reshape(128, 256).astype(jnp.bfloat16)

    for n in range(4):
        sib_copies[n].wait_recv()
        total = (part[n] + sib_in[n].astype(jnp.float32)).astype(jnp.bfloat16)
        regroup[n * 64:n * 64 + 32, :] = total[:, 0:quarter]
        regroup[n * 64 + 32:n * 64 + 64, :] = total[:, quarter:]
    unit[...] = jnp.dot(spread[...], regroup[...], preferred_element_type=jnp.float32).astype(jnp.bfloat16)

    def unit_of(ee, zz, yy):
        return unit.at[pl.ds(pl.multiple_of(((yy * 4 + zz) * 2 + ee) * 16, 16), 16), :]

    unit_copies = []
    for de, dz, dy in others:
        index = de * 8 + dz * 2 + dy
        copy = remote(
            unit_of((s + de) % 2, partner(dz), (y + dy) % 2), unit_in.at[index],
            r2_send.at[index], r2_recv.at[index], other_device(de, dz, dy),
        )
        copy.start()
        unit_copies.append(copy)
    sends += unit_copies

    for n in range(4):
        columns = pl.ds(n * pair, pair)
        some = rows[:, columns]
        down_out[0, :, columns] = lax.dot_general(
            hidden_pad, some, (((0,), (0,)), ((), ())), preferred_element_type=jnp.float32
        ).astype(jnp.bfloat16)
        inner = lax.dot_general(
            some, both_pad, (((0,), (0,)), ((), ())), preferred_element_type=jnp.float32
        ).astype(jnp.bfloat16)
        gate_out[0, columns, :] = inner[:, 0:128]
        up_out[0, columns, :] = inner[:, 128:256]

    for copy in unit_copies:
        copy.wait_recv()
    for de in range(2):
        if de == 0:
            result = unit[pl.ds(pl.multiple_of(((y * 4 + z) * 2 + s) * 16, 16), 16), :].astype(jnp.float32)
        else:
            result = unit_in[8].astype(jnp.float32)
        for index in range(1, 8):
            result = result + unit_in[de * 8 + index].astype(jnp.float32)
        final_out[pl.ds(pl.multiple_of(((s + de) % 2) * 16, 16), 16), :] = result.astype(jnp.bfloat16)
    for copy in sends:
        copy.wait_send()


def finish_kernel(final_ref, gate_ref, up_ref, down_ref, rows_out, gate_out, up_out, down_out, lines, sem, line_sem):
    copies = []
    depth = gate_ref.shape[1] // 4
    lanes = down_ref.shape[1] // 4
    for n in range(4):
        some = pl.ds(n * depth, depth)
        few = pl.ds(n * lanes, lanes)
        copies += [
            pltpu.make_async_copy(gate_ref.at[:, some, :], gate_out.at[:, some, :], sem.at[n]),
            pltpu.make_async_copy(up_ref.at[:, some, :], up_out.at[:, some, :], sem.at[4 + n]),
            pltpu.make_async_copy(down_ref.at[:, few, :], down_out.at[:, few, :], sem.at[8 + n]),
        ]
    for copy in copies:
        copy.start()
    quarter = final_ref.shape[1]
    final = final_ref[...].astype(jnp.float32)
    for e in range(2):
        for g in range(8):
            start = e * 16 + g * 2
            lines[0, 0, e, :, g * quarter:(g + 1) * quarter] = final[start:start + 2, :].astype(jnp.bfloat16)
    line_copy = pltpu.make_async_copy(lines, rows_out, line_sem)
    line_copy.start()
    for copy in copies:
        copy.wait()
    line_copy.wait()


def kernel_body(x_rows, cot_rows, counts, w_gate, w_up, w_down, kept_blocks, block_rank):
    width = x_rows.shape[4]
    quarter = width // 8
    pair = width // 4

    vmem = pl.BlockSpec(memory_space=pltpu.VMEM)
    hbm = pl.BlockSpec(memory_space=pltpu.HBM)
    anywhere = pl.BlockSpec(memory_space=pl.ANY)
    smem = pl.BlockSpec(memory_space=pltpu.SMEM)
    held = [
        pltpu.with_memory_space_constraint(a, pltpu.HBM) for a in (x_rows, cot_rows, counts, w_gate, w_up, w_down)
    ]
    bf16, f32 = jnp.bfloat16, jnp.float32
    dma = pltpu.SemaphoreType.DMA
    final_rows, grad_gate, grad_up, grad_down = pl.pallas_call(
        exchange_kernel,
        out_shape=(
            jax.ShapeDtypeStruct((32, quarter), bf16),
            jax.ShapeDtypeStruct(w_gate.shape, bf16),
            jax.ShapeDtypeStruct(w_up.shape, bf16),
            jax.ShapeDtypeStruct(w_down.shape, bf16),
        ),
        in_specs=[hbm, hbm, hbm, smem, smem, hbm, hbm, hbm],
        out_specs=(vmem, vmem, vmem, vmem),
        scratch_shapes=[
            pltpu.VMEM((2,) + x_rows.shape[2:], bf16),
            pltpu.SMEM(counts.shape, jnp.int32),
            pltpu.VMEM((2, 32, quarter), bf16),
            pltpu.VMEM((4, 256, quarter), bf16),
            pltpu.VMEM((256, 256), bf16),
            pltpu.VMEM((64, 64), bf16),
            pltpu.VMEM((256, 256), bf16),
            pltpu.VMEM((128, width), bf16),
            pltpu.VMEM((width, 384), bf16),
            pltpu.VMEM((256, width), bf16),
            pltpu.VMEM((128, width), bf16),
            pltpu.VMEM((64, 256), f32),
            pltpu.VMEM((64, 128), f32),
            pltpu.VMEM((4, 32, pair), bf16),
            pltpu.VMEM((4, 32, pair), bf16),
            pltpu.VMEM((4, 32, pair), f32),
            pltpu.VMEM((256, quarter), bf16),
            pltpu.VMEM((256, quarter), bf16),
            pltpu.VMEM((16, 16, quarter), bf16),
            dma((8,)), dma((8,)), dma((8,)), dma((8,)), dma((16,)), dma((16,)),
            dma((4,)), dma((4,)), dma((16,)), dma((16,)), dma((3,)), dma((3,)),
        ],
        compiler_params=pltpu.CompilerParams(
            collective_id=0, has_side_effects=True, vmem_limit_bytes=32 * 1024 * 1024
        ),
        name="expert_backward",
    )(*held[:3], kept_blocks, block_rank, *held[3:])
    return pl.pallas_call(
        finish_kernel,
        out_shape=tuple(jax.ShapeDtypeStruct(a.shape, bf16) for a in (x_rows, w_gate, w_up, w_down)),
        in_specs=[vmem, anywhere, anywhere, anywhere],
        out_specs=(anywhere, anywhere, anywhere, anywhere),
        scratch_shapes=[pltpu.VMEM(x_rows.shape, bf16), dma((12,)), dma(())],
        compiler_params=pltpu.CompilerParams(vmem_limit_bytes=16 * 1024 * 1024),
        name="write_outputs",
    )(final_rows, grad_gate, grad_up, grad_down)


def solution(mesh):
    in_specs = (
        P("expert", "dp", None, None, None),
        P("expert", "dp", None, None, None),
        P(None, "dp", None),
        P("expert", None, "dp"),
        P("expert", None, "dp"),
        P("expert", "dp", None),
        P("expert"),
        P("expert", "dp"),
    )
    out_specs = (
        P("expert", "dp", None, None, None),
        P("expert", None, "dp"),
        P("expert", None, "dp"),
        P("expert", "dp", None),
    )
    small = mesh.shape["expert"] == 2 and mesh.shape["dp"] == 16
    return jax.shard_map(kernel_body if small else body, mesh=mesh, in_specs=in_specs, out_specs=out_specs, check_vma=False)
```
